128 devices in a mesh: dp: 16 (over z, y), tensor: 8 (over x, core).
Axes of the slice: x: 4, y: 4, z: 4, core: 2. Of those that a mesh axis runs over, the one named last changes fastest.
Arguments:
- hidden: bfloat16 [256, 4, 8192], P('dp', None, 'tensor'), may hold values from -500 to 500
- norm_gain: bfloat16 [8192], replicated, may hold values from 0.099609375 to 1.8984375
- w_query: bfloat16 [8192, 8192], P(None, 'tensor'), may hold values from -0.0625 to 0.0625
- w_keyval: bfloat16 [2, 8192, 1024], P(None, None, 'tensor'), may hold values from -0.0625 to 0.0625
- b_query: bfloat16 [8192], P('tensor'), may hold values from -8 to 8
- b_keyval: bfloat16 [2, 1024], P(None, 'tensor'), may hold values from -3 to 3
- cache: bfloat16 [2, 4096, 64, 1024], P(None, 'dp', None, 'tensor'), may hold values from -32 to 32
- page_table: int32 [256, 16], P('dp'), may hold values from 0 to 255, as said below
- context: int32 [256], P('dp'), may hold values from 256 to 1024, as said below
- remaining: int32 [256], P('dp'), may hold values from 0 to 4
- move_to: int32 [256], P('dp'), may hold values from 0 to 255, as said below
Outputs:
- attended: bfloat16 [256, 4, 8192], P('dp', None, 'tensor')
- new_keyval: bfloat16 [2, 256, 4, 1024], P(None, 'dp', None, 'tensor')
- arrived: bfloat16 [2, 64, 1024, 1024], P(None, 'dp', None, 'tensor')
The draws below stay inside these ranges and needn't reach their ends.
Inputs may be any that keep to these rules, and one draw needn't show every extreme that they name: move_to is a permutation that is its own inverse. Each pair it swaps lies on two different dp ranks (the rank of slot g is g // 16) and holds one sample with remaining > 0 and one with remaining 0. At most 2 live samples move from one rank to one other rank, at most 4 leave one rank and at most 4 arrive at one rank; each of these bounds is reached in every draw. `context`: the largest value, 1024, is taken on every dp rank. `page_table`: counted from the start of its rank's block of 256 pages of cache; within one rank each page belongs to one sample.
All inputs are finite; a program needn't handle non-finite values.
Results may differ from the reference program's by a relative error of at most 0.0072.
Values may be sent and summed in bfloat16 or wider, within the bound.
No kernel may reach another device: no remote copies, remote signals or barrier semaphores. Data moves between devices by JAX's collectives and lax.ppermute only.
A program may use at most 192 MiB of HBM per device.

```python
import math
import jax
import jax.numpy as jnp
from jax import lax

D = 8192
HEADS = 64
KVH = 8
HD = 128
STEPS = 4
SLOTS = 16
PAGES = 16
PAGE = 64
CAP = 2
ARR = 4
CTX = 1024
SAMPLES = 256


def shared_directions(key):
    full_key = jax.random.fold_in(key, 103)
    full_signs = jax.random.randint(full_key, (KVH, HD), 0, 2).astype(jnp.float32) * 2.0 - 1.0
    return full_signs


def migration_plan(key):
    key = jax.random.fold_in(key, 107)
    dp_ranks = SAMPLES // SLOTS
    half_count = dp_ranks // 2
    subkeys = jax.random.split(key, 5)
    rank_order = jax.random.permutation(subkeys[0], dp_ranks).astype(jnp.int32)
    busy_ranks = rank_order[:half_count]
    drained = rank_order[half_count:]
    shuffles = jax.vmap(lambda sub_key: jax.random.permutation(sub_key, SLOTS))(jax.random.split(subkeys[1], dp_ranks)).astype(jnp.int32)
    row_ids = jnp.arange(dp_ranks, dtype=jnp.int32)[:, None]
    slot_range = jnp.broadcast_to(jnp.arange(SLOTS, dtype=jnp.int32)[None, :], (dp_ranks, SLOTS))
    position = jnp.zeros((dp_ranks, SLOTS), jnp.int32).at[row_ids, shuffles].set(slot_range)
    lengths = jax.random.randint(subkeys[2], (dp_ranks, SLOTS), 1, STEPS + 1)
    coin_flips = jax.random.randint(subkeys[3], (dp_ranks, SLOTS), 0, 2)
    is_busy = jnp.zeros((dp_ranks,), jnp.int32).at[busy_ranks].set(1)[:, None]
    drained_left = jnp.where((position < 2 * CAP) | (coin_flips == 0), 0, lengths)
    steps_left = jnp.where(is_busy == 1, lengths, drained_left)
    steps_left = jnp.where((is_busy == 1) & (position == 2 * CAP), STEPS, steps_left)
    counts = jax.random.randint(subkeys[4], (half_count, 2), 0, CAP + 1)
    counts = counts.at[0, 0].set(CAP).at[0, 1].set(CAP).at[1, 0].set(CAP)
    lane_ids = jnp.arange(CAP, dtype=jnp.int32)
    partner = drained[(jnp.arange(half_count)[:, None] + jnp.arange(2)[None, :]) % half_count]
    source_rank = jnp.broadcast_to(busy_ranks[:, None, None], (half_count, 2, CAP))
    dest_rank = jnp.broadcast_to(partner[:, :, None], (half_count, 2, CAP))
    column = jnp.broadcast_to(jnp.arange(2, dtype=jnp.int32)[None, :, None] * CAP + lane_ids[None, None, :], (half_count, 2, CAP))
    source = source_rank * SLOTS + shuffles[source_rank, column]
    dest_ids = dest_rank * SLOTS + shuffles[dest_rank, column]
    in_use = lane_ids[None, None, :] < counts[:, :, None]
    source = jnp.where(in_use, source, SAMPLES).reshape(-1)
    dest_ids = jnp.where(in_use, dest_ids, SAMPLES).reshape(-1)
    sample_ids = jnp.arange(SAMPLES, dtype=jnp.int32)
    targets = sample_ids.at[source].set(dest_ids, mode='drop').at[dest_ids].set(source, mode='drop')
    return (steps_left.reshape(-1).astype(jnp.int32), targets.astype(jnp.int32))


def draw_remaining(key, part):
    steps_left, targets = migration_plan(key)
    return steps_left


def draw_move_to(key, part):
    steps_left, targets = migration_plan(key)
    return targets


def draw_context(key, part):
    key = jax.random.fold_in(key, 11)
    subkeys = jax.random.split(key, 2)
    dp_ranks = SAMPLES // SLOTS
    lengths = jax.random.randint(subkeys[0], (SAMPLES,), CTX // 4, CTX + 1)
    longest = jax.random.randint(subkeys[1], (dp_ranks,), 0, SLOTS) + jnp.arange(dp_ranks, dtype=jnp.int32) * SLOTS
    return lengths.at[longest].set(CTX).astype(jnp.int32)


def draw_page_table(key, part):
    key = jax.random.fold_in(key, 13)
    dp_ranks = SAMPLES // SLOTS
    shuffled = jax.vmap(lambda sub_key: jax.random.permutation(sub_key, SLOTS * PAGES))(jax.random.split(key, dp_ranks))
    return shuffled.reshape(SAMPLES, PAGES).astype(jnp.int32)


def draw_hidden(key, part):
    key = jax.random.fold_in(key, 17)
    subkeys = jax.random.split(key, 3)
    shape = (SAMPLES, STEPS, D)
    row_scale = jnp.exp(jax.random.uniform(subkeys[1], (SAMPLES, STEPS, 1), jnp.float32, 0.0, math.log(10.0)))
    column_scale = jnp.exp(jax.random.uniform(subkeys[2], (1, 1, D), jnp.float32, 0.0, math.log(10.0)))
    drawn = jax.random.truncated_normal(subkeys[0], -4.0, 4.0, shape, jnp.float32)
    return (drawn * row_scale * column_scale).astype(jnp.bfloat16)


def draw_b_query(key, part):
    full_dir = shared_directions(key)
    key = jax.random.fold_in(key, 19)
    repeat = HEADS // KVH
    full_part = jnp.repeat(full_dir, repeat, axis=0).reshape(-1)
    drawn = 0.7 * full_part + 0.3 * jax.random.truncated_normal(key, -4.0, 4.0, (HEADS * HD,), jnp.float32)
    return drawn.astype(jnp.bfloat16)


def draw_b_keyval(key, part):
    full_dir = shared_directions(key)
    key = jax.random.fold_in(key, 23)
    jitter = jax.random.truncated_normal(key, -4.0, 4.0, (2, KVH * HD), jnp.float32)
    key_half = 0.7 * full_dir.reshape(-1) + 0.3 * jitter[0]
    value_half = 0.6 * jitter[1]
    return jnp.stack([key_half, value_half]).astype(jnp.bfloat16)


def draw_cache(key, part):
    key = jax.random.fold_in(key, 29)
    subkeys = jax.random.split(key, 1)
    page_total = SAMPLES * PAGES
    width = KVH * HD
    drawn = jax.random.truncated_normal(subkeys[0], -6.0, 6.0, (2, page_total, PAGE, width), jnp.float32)
    return drawn.astype(jnp.bfloat16)


def levels(stream_key, shape, shards, least, high):
    factor_of, own = 1.0, jax.random.fold_in(stream_key, 6)
    for dim, parts in shards:
        draws = jnp.exp(jax.random.uniform(jax.random.fold_in(own, dim), (parts,), jnp.float32, least / len(shards), high / len(shards)))
        factor_of = factor_of * jnp.repeat(draws, shape[dim] // parts).reshape([-1 if axis == dim else 1 for axis in range(len(shape))])
    return factor_of


def normal_values(key, shape, scale, limit, pieces=(), kind=jnp.bfloat16):
    gain = levels(key, shape, pieces, -0.22, 0.18) if pieces else 1.0
    values = jax.random.normal(key, shape, jnp.float32) * scale * gain
    return jnp.minimum(jnp.maximum(values, -limit), limit).astype(kind)


def setup_inputs(seed: int = 0) -> dict:
    key_list = jax.random.split(jax.random.key(seed), 12)
    hidden = draw_hidden(jax.random.fold_in(key_list[11], 71), 0)
    norm_gain = jnp.clip(1.0 + 0.18 * jax.random.normal(key_list[1], (D,), jnp.float32), 0.099609375, 1.8984375).astype(jnp.bfloat16)
    w_query = normal_values(key_list[2], (D, HEADS * HD), D ** -0.5, 0.0625, ((1, 8),))
    w_keyval = normal_values(key_list[3], (2, D, KVH * HD), D ** -0.5, 0.0625, ((2, 8),))
    b_query = draw_b_query(jax.random.fold_in(key_list[11], 71), 0)
    b_keyval = draw_b_keyval(jax.random.fold_in(key_list[11], 71), 0)
    cache = draw_cache(jax.random.fold_in(key_list[11], 71), 0)
    page_table = draw_page_table(jax.random.fold_in(key_list[11], 71), 0)
    context = draw_context(jax.random.fold_in(key_list[11], 71), 0)
    remaining = draw_remaining(jax.random.fold_in(key_list[11], 71), 0)
    move_to = draw_move_to(jax.random.fold_in(key_list[11], 71), 0)
    return dict(hidden=hidden, norm_gain=norm_gain, w_query=w_query, w_keyval=w_keyval, b_query=b_query, b_keyval=b_keyval, cache=cache, page_table=page_table, context=context, remaining=remaining, move_to=move_to)


rope_base = 1000000.0
norm_eps = 1e-06
masked_score = -1e+30

def rotate(values, positions):
    half_width = values.shape[-1] // 2
    inverse = rope_base ** (-(jnp.arange(half_width, dtype=jnp.float32) * (2.0 / values.shape[-1])))
    angles = positions.astype(jnp.float32)[:, :, None] * inverse[None, None, :]
    cosine = jnp.cos(angles)[:, :, None, :]
    sine_table = jnp.sin(angles)[:, :, None, :]
    first_half = values[..., :half_width]
    second = values[..., half_width:]
    return jnp.concatenate([first_half * cosine - second * sine_table, second * cosine + first_half * sine_table], axis=-1)

def project(hidden_rows, norm_gain, w_query, w_keyval, b_query, b_keyval, context_here):
    item_count, step_count, model_width = hidden_rows.shape
    flat_rows = hidden_rows.reshape(item_count * step_count, model_width).astype(jnp.float32)
    row_scale = lax.rsqrt(lax.optimization_barrier(jnp.mean(flat_rows * flat_rows, axis=1)) + norm_eps)[:, None]
    normed = (flat_rows * norm_gain.astype(jnp.float32)[None, :]).astype(jnp.bfloat16)
    query_sum = jnp.dot(normed, w_query, preferred_element_type=jnp.float32)
    key_sum = jnp.dot(normed, w_keyval[0], preferred_element_type=jnp.float32)
    value_sum = jnp.dot(normed, w_keyval[1], preferred_element_type=jnp.float32)
    positions = context_here[:, None] + jnp.arange(step_count, dtype=jnp.int32)[None, :]
    query_heads = (query_sum * row_scale + b_query.astype(jnp.float32)[None, :]).reshape(item_count, step_count, -1, HD)
    key_heads = (key_sum * row_scale + b_keyval[0].astype(jnp.float32)[None, :]).reshape(item_count, step_count, -1, HD)
    value_heads = (value_sum * row_scale + b_keyval[1].astype(jnp.float32)[None, :]).reshape(item_count, step_count, -1, HD)
    return (rotate(query_heads, positions).astype(jnp.bfloat16), rotate(key_heads, positions).astype(jnp.bfloat16), value_heads.astype(jnp.bfloat16))

def attend(query_heads, key_heads, value_heads, key_old, value_old, context_here, left_here):
    item_count, step_count, head_count, width = query_heads.shape
    groups = key_heads.shape[2]
    grouped = query_heads.reshape(item_count, step_count, groups, head_count // groups, width).astype(jnp.float32)
    score_scale = 1.0 / math.sqrt(width)
    old_scores = jnp.einsum('nsgrd,npgd->nsgrp', grouped, key_old.astype(jnp.float32)) * score_scale
    visible = jnp.arange(key_old.shape[1], dtype=jnp.int32)[None, :] < context_here[:, None]
    old_scores = jnp.where(visible[:, None, None, None, :], old_scores, masked_score)
    new_scores = jnp.einsum('nsgrd,ntgd->nsgrt', grouped, key_heads.astype(jnp.float32)) * score_scale
    causal = jnp.arange(step_count)[None, :] <= jnp.arange(step_count)[:, None]
    new_scores = jnp.where(causal[None, :, None, None, :], new_scores, masked_score)
    top_score = jnp.maximum(lax.optimization_barrier(jnp.max(old_scores, axis=-1)), lax.optimization_barrier(jnp.max(new_scores, axis=-1)))[..., None]
    old_exp = jnp.exp(old_scores - top_score)
    new_exp = jnp.exp(new_scores - top_score)
    totals = lax.optimization_barrier(jnp.sum(old_exp, axis=-1, keepdims=True)) + lax.optimization_barrier(jnp.sum(new_exp, axis=-1, keepdims=True))
    old_weights = (old_exp / totals).astype(jnp.bfloat16)
    new_weights = (new_exp / totals).astype(jnp.bfloat16)
    mixture = jnp.einsum('nsgrp,npgd->nsgrd', old_weights.astype(jnp.float32), value_old.astype(jnp.float32))
    mixture = mixture + jnp.einsum('nsgrt,ntgd->nsgrd', new_weights.astype(jnp.float32), value_heads.astype(jnp.float32))
    live_steps = jnp.arange(step_count, dtype=jnp.int32)[None, :] < left_here[:, None]
    mixture = jnp.where(live_steps[:, :, None, None, None], mixture, 0.0)
    return mixture.reshape(item_count, step_count, head_count * width).astype(jnp.bfloat16)

def reference(hidden, norm_gain, w_query, w_keyval, b_query, b_keyval, cache, page_table, context, remaining, move_to):
    dp_ranks = SAMPLES // SLOTS
    pool_size = SLOTS * PAGES

    def one_rank(dp_rank):
        first_row = (dp_rank * SLOTS).astype(jnp.int32)
        hidden_rows = lax.dynamic_slice_in_dim(hidden, first_row, SLOTS, 0)
        context_here = lax.dynamic_slice_in_dim(context, first_row, SLOTS, 0)
        left_here = lax.dynamic_slice_in_dim(remaining, first_row, SLOTS, 0)
        table_rows = lax.dynamic_slice_in_dim(page_table, first_row, SLOTS, 0)
        pool_here = lax.dynamic_slice_in_dim(cache, (dp_rank * pool_size).astype(jnp.int32), pool_size, 1)
        query_heads, key_heads, value_heads = project(hidden_rows, norm_gain, w_query, w_keyval, b_query, b_keyval, context_here)
        old_cache = jnp.take(pool_here, table_rows.reshape(-1), axis=1).reshape(2, SLOTS, CTX, KVH, HD)
        mixture = attend(query_heads, key_heads, value_heads, old_cache[0], old_cache[1], context_here, left_here)
        live_steps = jnp.arange(STEPS, dtype=jnp.int32)[None, :] < left_here[:, None]
        fresh_kv = jnp.stack([key_heads, value_heads]).reshape(2, SLOTS, STEPS, KVH * HD)
        fresh_kv = jnp.where(live_steps[None, :, :, None], fresh_kv, jnp.zeros_like(fresh_kv))
        return (mixture, fresh_kv)
    home_out, home_kv = lax.map(one_rank, jnp.arange(dp_ranks, dtype=jnp.int32))
    home_out = home_out.reshape(SAMPLES, STEPS, HEADS * HD)
    home_kv = jnp.moveaxis(home_kv, 1, 0).reshape(2, SAMPLES, STEPS, KVH * HD)
    attended = jnp.zeros_like(home_out).at[move_to].set(home_out)
    new_keyval = jnp.zeros_like(home_kv).at[:, move_to].set(home_kv)
    sample_ids = jnp.arange(SAMPLES, dtype=jnp.int32)
    inverse = jnp.zeros((SAMPLES,), jnp.int32).at[move_to].set(sample_ids)
    arrival_flags = (inverse // SLOTS != sample_ids // SLOTS) & (remaining[inverse] > 0)
    flag_grid = arrival_flags.reshape(dp_ranks, SLOTS).astype(jnp.int32)
    order_grid = jnp.cumsum(flag_grid, axis=1) - 1
    target = jnp.where(flag_grid > 0, jnp.arange(dp_ranks, dtype=jnp.int32)[:, None] * ARR + order_grid, dp_ranks * ARR).reshape(-1)
    source = jnp.zeros((dp_ranks * ARR,), jnp.int32).at[target].set(inverse, mode='drop')
    filled = jnp.zeros((dp_ranks * ARR,), jnp.int32).at[target].set(1, mode='drop')
    page_ids = page_table[source] + (source // SLOTS)[:, None] * pool_size
    taken_pages = jnp.take(cache, page_ids.reshape(-1), axis=1).reshape(2, dp_ranks * ARR, CTX, KVH * HD)
    keep_mask = (filled[:, None] > 0) & (jnp.arange(CTX, dtype=jnp.int32)[None, :] < context[source][:, None])
    arrived = jnp.where(keep_mask[None, :, :, None], taken_pages, jnp.zeros_like(taken_pages))
    return (attended, new_keyval, arrived)
```

```python
import math

import jax
import jax.numpy as jnp
from jax import lax
from jax.experimental import pallas as pl
from jax.experimental.pallas import tpu as pltpu
from jax.sharding import PartitionSpec as P

HD = 128
ARR = 4
CAP = 2
TILE = 16

rope_base = 1000000.0
norm_eps = 1e-06
masked_score = -1e30


def pack_pages(page_table, context, remaining, move_to, rank, cache, ranks):
    slots, pages = page_table.shape
    page = cache.shape[2]
    tiles = page // TILE
    pool = cache.reshape(2, cache.shape[1], tiles, TILE, HD)
    last = ARR * 2 * tiles

    def kernel(table, ctx, left, goal, me, pool_ref, out_ref, list_ref, sems):
        def note(b, count):
            leaves = jnp.logical_and(left[b] > 0, goal[b] != me[0] * slots + b)

            @pl.when(leaves)
            def _():
                list_ref[jnp.minimum(count, ARR - 1)] = b

            return count + leaves.astype(jnp.int32)

        count = lax.fori_loop(0, slots, note, jnp.int32(0))
        count = jnp.minimum(count, ARR)

        def copies(m, j):
            b = list_ref[m]
            return [
                pltpu.make_async_copy(
                    pool_ref.at[kind, table[b * pages + j]],
                    out_ref.at[j, pl.ds((m * 2 + kind) * tiles, tiles)],
                    sems.at[m],
                )
                for kind in range(2)
            ]

        def used(m):
            return lax.div(ctx[list_ref[m]] + page - 1, page)

        def start(m, carry):
            def one(j, inner):
                for copy in copies(m, j):
                    copy.start()
                return inner

            return lax.fori_loop(0, used(m), one, carry)

        lax.fori_loop(0, count, start, 0)
        lane = lax.broadcasted_iota(jnp.int32, (TILE, HD), 1)
        note_tile = jnp.full((TILE, HD), 512, jnp.int32)
        for m in range(ARR):
            place = jnp.where(m < count, goal[list_ref[m]], 512) if m else jnp.where(count > 0, goal[list_ref[0]], 512)
            note_tile = jnp.where(lane == m, place, note_tile)
        note_tile = note_tile.astype(jnp.float32).astype(jnp.bfloat16)
        for j in range(ranks):
            out_ref[j, last] = note_tile
        row = lax.broadcasted_iota(jnp.int32, (tiles, TILE, HD), 0) * TILE + lax.broadcasted_iota(
            jnp.int32, (tiles, TILE, HD), 1
        )

        def finish(m, carry):
            full = used(m)

            def one(j, inner):
                for copy in copies(m, j):
                    copy.wait()
                return inner

            lax.fori_loop(0, full, one, 0)
            rest = ctx[list_ref[m]] - (full - 1) * page
            for kind in range(2):
                at = pl.ds((m * 2 + kind) * tiles, tiles)
                edge = out_ref[full - 1, at]
                out_ref[full - 1, at] = jnp.where(row < rest, edge, jnp.zeros_like(edge))

            def clear(j, inner):
                at = pl.ds(m * 2 * tiles, 2 * tiles)
                out_ref[j, at] = jnp.zeros((2 * tiles, TILE, HD), jnp.bfloat16)
                return inner

            return lax.fori_loop(full, pages, clear, carry)

        lax.fori_loop(0, count, finish, 0)

    return pl.pallas_call(
        kernel,
        grid_spec=pltpu.PrefetchScalarGridSpec(
            num_scalar_prefetch=5,
            grid=(1,),
            in_specs=[pl.BlockSpec(memory_space=pl.ANY)],
            out_specs=pl.BlockSpec((ranks, last + 1, TILE, HD), lambda i, *_: (0, 0, 0, 0)),
            scratch_shapes=[pltpu.SMEM((ARR,), jnp.int32), pltpu.SemaphoreType.DMA((ARR,))],
        ),
        out_shape=jax.ShapeDtypeStruct((ranks, last + 1, TILE, HD), jnp.bfloat16),
        compiler_params=pltpu.CompilerParams(vmem_limit_bytes=24 * 1024 * 1024),
        name="pack_pages",
    )(page_table.reshape(-1), context, remaining, move_to, rank.reshape(1), pool)


def relay_pages(source, received):
    ranks, rows = received.shape[:2]
    span = (rows - 1) // ARR

    def kernel(src, got_ref, out_ref, sem):
        def copy(t):
            k = src[t]
            return pltpu.make_async_copy(
                got_ref.at[lax.div(k, ARR), pl.ds(lax.rem(k, ARR) * span, span)],
                out_ref.at[lax.div(t, ARR), pl.ds(lax.rem(t, ARR) * span, span)],
                sem,
            )

        def start(t, carry):
            @pl.when(src[t] >= 0)
            def _():
                copy(t).start()

            return carry

        def clear(t, carry):
            @pl.when(src[t] < 0)
            def _():
                at = pl.ds(lax.rem(t, ARR) * span, span)
                out_ref[lax.div(t, ARR), at] = jnp.zeros((span, TILE, HD), jnp.bfloat16)

            return carry

        def finish(t, carry):
            @pl.when(src[t] >= 0)
            def _():
                copy(t).wait()

            return carry

        lax.fori_loop(0, ranks * ARR, start, 0)
        lax.fori_loop(0, ranks * ARR, clear, 0)
        lax.fori_loop(0, ranks * ARR, finish, 0)

    return pl.pallas_call(
        kernel,
        grid_spec=pltpu.PrefetchScalarGridSpec(
            num_scalar_prefetch=1,
            grid=(1,),
            in_specs=[pl.BlockSpec(memory_space=pl.ANY)],
            out_specs=pl.BlockSpec((ranks, rows - 1, TILE, HD), lambda i, *_: (0, 0, 0, 0)),
            scratch_shapes=[pltpu.SemaphoreType.DMA(())],
        ),
        out_shape=jax.ShapeDtypeStruct((ranks, rows - 1, TILE, HD), jnp.bfloat16),
        compiler_params=pltpu.CompilerParams(vmem_limit_bytes=24 * 1024 * 1024),
        name="relay_pages",
    )(source, received)


def plan_relay(goals, slots, ranks):
    count = goals.shape[0]
    home = goals // slots
    before = (home[None, :] == home[:, None]) & (goals[None, :] < goals[:, None])
    order = jnp.sum(before.astype(jnp.int32), axis=1)
    target = home * ARR + order
    ids = jnp.arange(count, dtype=jnp.int32)
    hit = target[None, :] == jnp.arange(ranks * ARR, dtype=jnp.int32)[:, None]
    return jnp.max(jnp.where(hit, ids[None, :], -1), axis=1)


def project_attend(
    page_table, context, remaining, hidden_parts, gain, w_query, w_keyval, b_query, b_keyval, cos, sin, pick, cache
):
    slots, pages = page_table.shape
    parts, rows, depth = hidden_parts.shape
    steps = rows // slots
    page = cache.shape[2]
    width = w_query.shape[1]
    heads = width // HD
    span = pages * page
    total = span + HD
    sends = pick.shape[0]
    group = TILE // steps
    scale = 1.0 / math.sqrt(HD)
    per = slots // parts
    model_width = parts * depth

    def kernel(
        table, ctx, left, hid_ref, gain_ref, wq_ref, wkv_ref, bq_ref, bkv_ref, cos_ref, sin_ref, pick_ref, cache_ref,
        rows_ref, send_ref, acc, squares, old, query, mixed, sems,
    ):
        step = pl.program_id(0)

        def used(b):
            return jnp.where(left[b] > 0, lax.div(ctx[b] + page - 1, page), 0)

        def copy(b, j):
            return pltpu.make_async_copy(
                cache_ref.at[:, table[b * pages + j]], old.at[b, :, pl.ds(j * page, page)], sems.at[b]
            )

        for n in range(per):
            b = step * per + n

            def fetch(j, carry, b=b):
                copy(b, j).start()
                return carry

            def clear(j, carry, b=b):
                old[b, 1, pl.ds(j * page, page)] = jnp.zeros((page, HD), jnp.bfloat16)
                return carry

            lax.fori_loop(0, used(b), fetch, 0)
            lax.fori_loop(used(b), pages, clear, 0)

        part = hid_ref[0].astype(jnp.float32)
        normed = (part * gain_ref[0].astype(jnp.float32)).astype(jnp.bfloat16)
        square = jnp.sum(part * part, axis=1, keepdims=True)
        q_part = jnp.dot(normed, wq_ref[...], preferred_element_type=jnp.float32)
        k_part = jnp.dot(normed, wkv_ref[0], preferred_element_type=jnp.float32)
        v_part = jnp.dot(normed, wkv_ref[1], preferred_element_type=jnp.float32)

        @pl.when(step == 0)
        def _():
            acc[:, :width] = q_part
            acc[:, width : width + HD] = k_part
            acc[:, width + HD :] = v_part
            squares[...] = jnp.broadcast_to(square, squares.shape)

        @pl.when(step > 0)
        def _():
            acc[:, :width] += q_part
            acc[:, width : width + HD] += k_part
            acc[:, width + HD :] += v_part
            squares[...] += jnp.broadcast_to(square, squares.shape)

        @pl.when(step == parts - 1)
        def _():
            row_scale = lax.rsqrt(squares[:, :1] / model_width + norm_eps)
            cosine, sine = cos_ref[...], sin_ref[...]

            def rotate(x):
                return x * cosine + pltpu.roll(x, HD // 2, 1) * sine

            for h in range(heads):
                at = slice(h * HD, (h + 1) * HD)
                q = rotate(acc[:, at] * row_scale + bq_ref[:, at].astype(jnp.float32))
                for b in range(slots):
                    base = (b * heads + h) * steps
                    query[base : base + steps, :] = q[b * steps : (b + 1) * steps, :]
            key = rotate(acc[:, width : width + HD] * row_scale + bkv_ref[0:1].astype(jnp.float32))
            value = acc[:, width + HD :] * row_scale + bkv_ref[1:2].astype(jnp.float32)
            key_new = key.astype(jnp.bfloat16)
            value_new = value.astype(jnp.bfloat16)
            row_of = lax.broadcasted_iota(jnp.int32, (rows, HD), 0)
            live_of = jnp.zeros((rows, HD), jnp.int32)
            for b in range(slots):
                live_of = jnp.where(row_of // steps == b, left[b], live_of)
            alive = row_of % steps < live_of
            mixed[:, width : width + HD] = jnp.where(alive, key, 0.0)
            mixed[:, width + HD :] = jnp.where(alive, value, 0.0)
            for b in range(slots):
                g = b // group
                old[b, 0, span : span + TILE] = key_new[g * TILE : (g + 1) * TILE]
                old[b, 1, span : span + TILE] = value_new[g * TILE : (g + 1) * TILE]
                old[b, 1, span + TILE :] = jnp.zeros((HD - TILE, HD), jnp.bfloat16)
            many = heads * steps
            col = lax.broadcasted_iota(jnp.int32, (many, total), 1)
            when = lax.broadcasted_iota(jnp.int32, (many, total), 0) % steps
            when_out = lax.broadcasted_iota(jnp.int32, (many, HD), 0) % steps

            for b in range(slots):
                def done(j, carry, b=b):
                    copy(b, j).wait()
                    return carry

                lax.fori_loop(0, used(b), done, 0)
                q = query[b * many : (b + 1) * many, :].astype(jnp.bfloat16)
                scores = (
                    lax.dot_general(q, old[b, 0], (((1,), (1,)), ((), ())), preferred_element_type=jnp.float32) * scale
                )
                fresh = col - (span + (b % group) * steps)
                seen = (col < ctx[b]) | ((fresh >= 0) & (fresh <= when))
                scores = jnp.where(seen, scores, masked_score)
                top = jnp.max(scores, axis=1, keepdims=True)
                weights = jnp.exp(scores - top)
                weights = weights / jnp.sum(weights, axis=1, keepdims=True)
                out = jnp.dot(weights.astype(jnp.bfloat16), old[b, 1], preferred_element_type=jnp.float32)
                out = jnp.where(when_out < left[b], out, 0.0)
                for h in range(heads):
                    mixed[b * steps : (b + 1) * steps, h * HD : (h + 1) * HD] = out[h * steps : (h + 1) * steps]

            done_rows = mixed[...].astype(jnp.bfloat16)
            rows_ref[...] = done_rows
            chosen = pick_ref[...] == lax.broadcasted_iota(jnp.int32, (sends, rows), 1)
            send_ref[...] = jnp.dot(
                chosen.astype(jnp.bfloat16), done_rows, preferred_element_type=jnp.float32
            ).astype(jnp.bfloat16)

    whole = lambda *shape: pl.BlockSpec(shape, lambda i, *_: (0,) * len(shape))
    wide = width + 2 * HD
    return pl.pallas_call(
        kernel,
        grid_spec=pltpu.PrefetchScalarGridSpec(
            num_scalar_prefetch=3,
            grid=(parts,),
            in_specs=[
                pl.BlockSpec((1, rows, depth), lambda i, *_: (i, 0, 0)),
                pl.BlockSpec((1, 1, depth), lambda i, *_: (i, 0, 0)),
                pl.BlockSpec((depth, width), lambda i, *_: (i, 0)),
                pl.BlockSpec((2, depth, HD), lambda i, *_: (0, i, 0)),
                whole(1, width),
                whole(2, HD),
                whole(rows, HD),
                whole(rows, HD),
                whole(sends, 1),
                pl.BlockSpec(memory_space=pl.ANY),
            ],
            out_specs=[whole(rows, wide), whole(sends, wide)],
            scratch_shapes=[
                pltpu.VMEM((rows, wide), jnp.float32),
                pltpu.VMEM((rows, HD), jnp.float32),
                pltpu.VMEM((slots, 2, total, HD), jnp.bfloat16),
                pltpu.VMEM((rows * heads, HD), jnp.float32),
                pltpu.VMEM((rows, wide), jnp.float32),
                pltpu.SemaphoreType.DMA((slots,)),
            ],
        ),
        out_shape=[
            jax.ShapeDtypeStruct((rows, wide), jnp.bfloat16),
            jax.ShapeDtypeStruct((sends, wide), jnp.bfloat16),
        ],
        compiler_params=pltpu.CompilerParams(vmem_limit_bytes=36 * 1024 * 1024),
        cost_estimate=pl.CostEstimate(
            flops=2 * rows * model_width * wide, bytes_accessed=32 * 1024 * 1024, transcendentals=rows * heads * total
        ),
        name="project_attend",
    )(
        page_table.reshape(-1), context, remaining, hidden_parts, gain.reshape(parts, 1, depth), w_query, w_keyval,
        b_query.reshape(1, width), b_keyval, cos, sin, pick.reshape(sends, 1), cache,
    )


def local(
    hidden, norm_gain, w_query, w_keyval, b_query, b_keyval, cache, page_table, context, remaining, move_to
):
    slots, steps, depth = hidden.shape
    ranks = lax.axis_size("dp")
    rank = lax.axis_index("dp").astype(jnp.int32)
    page = cache.shape[2]
    pages = page_table.shape[1]
    width = w_query.shape[1]
    rows = slots * steps
    ids = jnp.arange(slots, dtype=jnp.int32)

    sent = pack_pages(page_table, context, remaining, move_to, rank, cache, ranks)
    received = lax.all_to_all(sent, "dp", 0, 0, tiled=True)
    goals = received[:, -1, 0, :ARR].astype(jnp.int32).reshape(-1)
    relayed = relay_pages(plan_relay(goals, slots, ranks), received)
    landed = lax.all_to_all(relayed, "dp", 0, 0, tiled=True)
    arrived = landed.reshape(ranks, ARR, 2, page, HD).transpose(2, 1, 0, 3, 4).reshape(2, ARR, pages * page, HD)

    staying = move_to == ids + rank * slots
    leaving = jnp.logical_not(staying) & (remaining > 0)
    coming = jnp.logical_not(staying) & (remaining == 0)
    there = move_to // slots
    same = there[None, :] == there[:, None]
    leave_order = jnp.sum((same & leaving[None, :] & (ids[None, :] < ids[:, None])).astype(jnp.int32), axis=1)
    come_order = jnp.sum(
        (same & coming[None, :] & (move_to[None, :] < move_to[:, None])).astype(jnp.int32), axis=1
    )
    place = jnp.where(leaving, there * CAP + leave_order, -1)
    hit = place[None, :] == jnp.arange(ranks * CAP, dtype=jnp.int32)[:, None]
    slot_of = jnp.max(jnp.where(hit, ids[None, :], -1), axis=1)
    step_ids = jnp.arange(steps, dtype=jnp.int32)
    pick = jnp.where(slot_of[:, None] >= 0, slot_of[:, None] * steps + step_ids[None, :], -1).reshape(-1)

    half = HD // 2
    inverse = rope_base ** (-(jnp.arange(half, dtype=jnp.float32) * (2.0 / HD)))
    positions = (context[:, None] + step_ids[None, :]).reshape(-1).astype(jnp.float32)
    angles = positions[:, None] * inverse[None, :]
    cos, sin = jnp.cos(angles), jnp.sin(angles)
    cos = jnp.concatenate([cos, cos], axis=1)
    sin = jnp.concatenate([-sin, sin], axis=1)

    parts = lax.all_gather(hidden.reshape(rows, depth), "tensor", axis=0)
    mine, going = project_attend(
        page_table, context, remaining, parts, norm_gain, w_query, w_keyval, b_query, b_keyval, cos, sin, pick, cache
    )
    got = lax.all_to_all(going.reshape(ranks, CAP * steps, -1), "dp", 0, 0, tiled=True)
    everything = jnp.concatenate([mine, got.reshape(ranks * CAP * steps, -1)], axis=0)
    base = jnp.where(staying, ids * steps, jnp.where(coming, rows + (there * CAP + come_order) * steps, -steps))
    take = (base[:, None] + step_ids[None, :]).reshape(-1)
    chosen = (take[:, None] == jnp.arange(everything.shape[0], dtype=jnp.int32)[None, :]).astype(jnp.bfloat16)
    final = jnp.dot(chosen, everything, preferred_element_type=jnp.float32).astype(jnp.bfloat16)
    attended = final[:, :width].reshape(slots, steps, width)
    new_keyval = jnp.stack([final[:, width : width + HD], final[:, width + HD :]]).reshape(2, slots, steps, HD)
    return attended, new_keyval, arrived


def solution(mesh):
    in_specs = (
        P("dp", None, "tensor"),
        P(),
        P(None, "tensor"),
        P(None, None, "tensor"),
        P("tensor"),
        P(None, "tensor"),
        P(None, "dp", None, "tensor"),
        P("dp", None),
        P("dp"),
        P("dp"),
        P("dp"),
    )
    out_specs = (
        P("dp", None, "tensor"),
        P(None, "dp", None, "tensor"),
        P(None, "dp", None, "tensor"),
    )
    return jax.shard_map(local, mesh=mesh, in_specs=in_specs, out_specs=out_specs, check_vma=False)
```

```python
import math

import jax
import jax.numpy as jnp
from jax import lax
from jax.experimental import pallas as pl
from jax.experimental.pallas import tpu as pltpu
from jax.sharding import PartitionSpec as P

HD = 128
ARR = 4
CAP = 2
TILE = 16
STEPS = 4

rope_base = 1000000.0
norm_eps = 1e-06
masked_score = -1e30


def pack_pages(page_table, context, remaining, move_to, cache, ranks):
    slots, pages = page_table.shape
    page = cache.shape[2]
    tiles = page // TILE
    pool = cache.reshape(2, cache.shape[1], tiles, TILE, HD)
    last = ARR * 2 * tiles

    def kernel(
        table_hbm, ctx_hbm, left_hbm, goal_hbm, pool_ref, out_ref, table, ctx, left, goal, list_ref, stage, sems, small,
    ):
        reads = [
            pltpu.make_async_copy(src, dst, small.at[n])
            for n, (src, dst) in enumerate(
                ((table_hbm, table), (ctx_hbm, ctx), (left_hbm, left), (goal_hbm, goal))
            )
        ]
        for read in reads:
            read.start()
        for read in reads:
            read.wait()
        first = lax.axis_index("dp").astype(jnp.int32) * slots

        for m in range(ARR):
            list_ref[m] = 0
        count = jnp.int32(0)
        for b in range(slots):
            leaves = jnp.logical_and(left[b] > 0, goal[b] != first + b)
            list_ref[jnp.where(leaves, jnp.minimum(count, ARR - 1), ARR)] = b
            count = count + leaves.astype(jnp.int32)
        count = jnp.minimum(count, ARR)

        def used(m):
            return lax.div(ctx[list_ref[m]] + page - 1, page)

        def reads_of(m, j):
            b = list_ref[m]
            return [
                pltpu.make_async_copy(
                    pool_ref.at[kind, table[b, j]], stage.at[j, pl.ds((m * 2 + kind) * tiles, tiles)], sems.at[m]
                )
                for kind in range(2)
            ]

        def start(m, carry):
            def one(j, inner):
                for copy in reads_of(m, j):
                    copy.start()
                return inner

            return lax.fori_loop(0, used(m), one, carry)

        lax.fori_loop(0, count, start, 0)
        lane = lax.broadcasted_iota(jnp.int32, (TILE, HD), 1)
        note_tile = jnp.full((TILE, HD), 512, jnp.int32)
        for m in range(ARR):
            note_tile = jnp.where(lane == m, jnp.where(m < count, goal[list_ref[m]], 512), note_tile)
        note_tile = note_tile.astype(jnp.float32).astype(jnp.bfloat16)
        for j in range(ranks):
            stage[j, last] = note_tile

        def clear(m, carry):
            def one(j, inner):
                stage[j, pl.ds(m * 2 * tiles, 2 * tiles)] = jnp.zeros((2 * tiles, TILE, HD), jnp.bfloat16)
                return inner

            return lax.fori_loop(used(m), pages, one, carry)

        lax.fori_loop(0, count, clear, 0)
        row = lax.broadcasted_iota(jnp.int32, (tiles, TILE, HD), 0) * TILE + lax.broadcasted_iota(
            jnp.int32, (tiles, TILE, HD), 1
        )

        def finish(m, carry):
            full = used(m)

            def one(j, inner):
                for copy in reads_of(m, j):
                    copy.wait()
                return inner

            lax.fori_loop(0, full, one, 0)
            rest = ctx[list_ref[m]] - (full - 1) * page
            for kind in range(2):
                at = pl.ds((m * 2 + kind) * tiles, tiles)
                edge = stage[full - 1, at]
                stage[full - 1, at] = jnp.where(row < rest, edge, jnp.zeros_like(edge))
            return carry

        lax.fori_loop(0, count, finish, 0)
        out = pltpu.make_async_copy(stage, out_ref, sems.at[ARR])
        out.start()
        out.wait()

    hbm = pl.BlockSpec(memory_space=pltpu.HBM)
    return pl.pallas_call(
        kernel,
        in_specs=[hbm] * 5,
        out_specs=hbm,
        scratch_shapes=[
            pltpu.SMEM((slots, pages), jnp.int32),
            pltpu.SMEM((slots,), jnp.int32),
            pltpu.SMEM((slots,), jnp.int32),
            pltpu.SMEM((slots,), jnp.int32),
            pltpu.SMEM((ARR + 1,), jnp.int32),
            pltpu.VMEM((ranks, last + 1, TILE, HD), jnp.bfloat16),
            pltpu.SemaphoreType.DMA((ARR + 1,)),
            pltpu.SemaphoreType.DMA((4,)),
        ],
        out_shape=jax.ShapeDtypeStruct((ranks, last + 1, TILE, HD), jnp.bfloat16),
        compiler_params=pltpu.CompilerParams(vmem_limit_bytes=56 * 1024 * 1024),
        name="pack_pages",
    )(page_table, context, remaining, move_to, pool)


def relay_pages(source, received, going, take):
    ranks, rows = received.shape[:2]
    span = (rows - 1) // ARR
    more = going.shape[0]

    def kernel(src, got_ref, going_ref, take_ref, out_ref, tile_ref):
        for d in range(ranks):
            for a in range(ARR):
                k = src[d * ARR + a]
                place = jnp.maximum(k, 0)
                block = got_ref[place // ARR, pl.ds((place & (ARR - 1)) * span, span)]
                out_ref[d, a * span : (a + 1) * span] = jnp.where(k >= 0, block, jnp.zeros_like(block))
            for c in range(more):
                out_ref[d, ARR * span + c] = going_ref[c, d * TILE : (d + 1) * TILE]
        tile_ref[...] = jnp.broadcast_to(take_ref[...], tile_ref.shape)

    vmem = pl.BlockSpec(memory_space=pltpu.VMEM)
    return pl.pallas_call(
        kernel,
        in_specs=[pl.BlockSpec(memory_space=pltpu.SMEM), vmem, vmem, vmem],
        out_specs=[vmem, vmem],
        out_shape=[
            jax.ShapeDtypeStruct((ranks, ARR * span + more, TILE, HD), jnp.bfloat16),
            jax.ShapeDtypeStruct((take.shape[0], HD), jnp.int32),
        ],
        compiler_params=pltpu.CompilerParams(vmem_limit_bytes=16 * 1024 * 1024),
        name="relay_pages",
    )(source, received, going, take)


def plan_relay(goals, slots, ranks):
    count = goals.shape[0]
    home = goals // slots
    before = (home[None, :] == home[:, None]) & (goals[None, :] < goals[:, None])
    order = jnp.sum(before.astype(jnp.int32), axis=1)
    target = home * ARR + order
    ids = jnp.arange(count, dtype=jnp.int32)
    hit = target[None, :] == jnp.arange(ranks * ARR, dtype=jnp.int32)[:, None]
    return jnp.max(jnp.where(hit, ids[None, :], -1), axis=1)


def project_attend(
    page_table, context, remaining, origin, parts, gain, w_query, w_keyval, b_query, b_keyval, cos, sin, pick, cache
):
    slots, pages = page_table.shape
    count = len(parts)
    rows, depth = parts[0].shape
    steps = rows // slots
    page = cache.shape[2]
    width = w_query.shape[1]
    wide = width + 2 * HD
    heads = width // HD
    span = pages * page
    sends = pick.shape[0]
    chunks = wide // HD
    pair = 8 // steps
    scale = 1.0 / math.sqrt(HD)
    model_width = count * depth
    half = depth // 2

    def kernel(*refs):
        table, ctx, left, source = refs[:4]
        hid = refs[4 : 4 + count]
        (
            gain_ref, wq_hbm, wkv_hbm, bq_ref, bkv_ref, cos_ref, sin_ref, pick_ref, cache_ref,
            rows_ref, send_ref, wq, wkv, acc, old, query, fresh, mixed, weight_sems, sems,
        ) = refs[4 + count :]

        def weights_of(i, n):
            begin = pl.multiple_of(source[i] * depth + n * half, half)
            at = pl.ds(i * depth + n * half, half)
            sem = weight_sems.at[2 * i + n]
            return [
                pltpu.make_async_copy(wq_hbm.at[pl.ds(begin, half)], wq.at[at], sem),
                pltpu.make_async_copy(wkv_hbm.at[:, pl.ds(begin, half)], wkv.at[:, at], sem),
            ]

        for i in range(count):
            for n in range(2):
                for copy in weights_of(i, n):
                    copy.start()

        def used(b):
            return jnp.where(left[b] > 0, lax.div(ctx[b] + page - 1, page), 0)

        def copy_page(b, j):
            return pltpu.make_async_copy(
                cache_ref.at[:, table[b * pages + j]], old.at[b, :, pl.ds(j * page, page)], sems.at[b]
            )

        def fetch(b, carry):
            def one(j, inner):
                copy_page(b, j).start()
                return inner

            def clear(j, inner):
                old[b, 1, pl.ds(j * page, page)] = jnp.zeros((page, HD), jnp.bfloat16)
                return inner

            lax.fori_loop(0, used(b), one, 0)
            return lax.fori_loop(used(b), pages, clear, carry)

        lax.fori_loop(0, slots, fetch, 0)

        squares = jnp.zeros((rows, 1), jnp.float32)
        for i in range(count):
            for n in range(2):
                at = slice(n * half, (n + 1) * half)
                part = hid[i][:, at].astype(jnp.float32)
                normed = (part * gain_ref[source[i], :, at].astype(jnp.float32)).astype(jnp.bfloat16)
                squares += jnp.sum(part * part, axis=1, keepdims=True)
                for copy in weights_of(i, n):
                    copy.wait()
                at = slice(i * depth + n * half, i * depth + (n + 1) * half)
                sums = [
                    jnp.dot(normed, wq[at], preferred_element_type=jnp.float32),
                    jnp.dot(normed, wkv[0, at], preferred_element_type=jnp.float32),
                    jnp.dot(normed, wkv[1, at], preferred_element_type=jnp.float32),
                ]
                for lanes, part_sum in zip(
                    (slice(0, width), slice(width, width + HD), slice(width + HD, wide)), sums, strict=True
                ):
                    if i or n:
                        acc[:, lanes] += part_sum
                    else:
                        acc[:, lanes] = part_sum

        row_scale = lax.rsqrt(squares / model_width + norm_eps)
        cosine, sine = cos_ref[...], sin_ref[...]

        def rotate(x):
            return x * cosine + pltpu.roll(x, HD // 2, 1) * sine

        many = heads * 8
        for h in range(heads):
            at = slice(h * HD, (h + 1) * HD)
            q = rotate(acc[:, at] * row_scale + bq_ref[:, at].astype(jnp.float32))
            for p in range(rows // 8):
                query[p * many + h * 8 : p * many + (h + 1) * 8, :] = q[p * 8 : (p + 1) * 8, :]
        key = rotate(acc[:, width : width + HD] * row_scale + bkv_ref[0:1].astype(jnp.float32))
        value = acc[:, width + HD :] * row_scale + bkv_ref[1:2].astype(jnp.float32)
        fresh[0, :rows] = key.astype(jnp.bfloat16)
        fresh[1, :rows] = value.astype(jnp.bfloat16)
        fresh[:, rows:] = jnp.zeros((2, HD - rows, HD), jnp.bfloat16)
        row_of = lax.broadcasted_iota(jnp.int32, (rows, HD), 0)
        live_of = jnp.zeros((rows, HD), jnp.int32)
        for b in range(slots):
            live_of = jnp.where(row_of // steps == b, left[b], live_of)
        alive = row_of % steps < live_of
        mixed[:, width : width + HD] = jnp.where(alive, key, 0.0)
        mixed[:, width + HD :] = jnp.where(alive, value, 0.0)

        def await_pages(b, carry):
            def one(j, inner):
                copy_page(b, j).wait()
                return inner

            return lax.fori_loop(0, used(b), one, carry)

        lax.fori_loop(0, slots, await_pages, 0)

        col = lax.broadcasted_iota(jnp.int32, (many, span), 1)
        new_col = lax.broadcasted_iota(jnp.int32, (many, HD), 1)
        line = lax.broadcasted_iota(jnp.int32, (many, HD), 0) % 8
        line_one = lax.broadcasted_iota(jnp.int32, (many, 1), 0) % 8
        for p in range(slots // pair):
            members = range(p * pair, (p + 1) * pair)
            q = query[p * many : (p + 1) * many, :].astype(jnp.bfloat16)

            def mine(values, at):
                out = values[0]
                for n in range(1, pair):
                    out = jnp.where(at >= n * steps, values[n], out)
                return out

            wide_line = jnp.broadcast_to(line_one, (many, span))
            scores = mine(
                [
                    lax.dot_general(q, old[b, 0], (((1,), (1,)), ((), ())), preferred_element_type=jnp.float32)
                    for b in members
                ],
                wide_line,
            )
            limit = mine([jnp.full((many, 1), ctx[b], jnp.int32) for b in members], line_one)
            scores = jnp.where(col < limit, scores * scale, masked_score)
            late = lax.dot_general(q, fresh[0], (((1,), (1,)), ((), ())), preferred_element_type=jnp.float32)
            since = new_col - p * 8
            seen = (since >= (line // steps) * steps) & (since <= line)
            late = jnp.where(seen, late * scale, masked_score)
            top = jnp.maximum(jnp.max(scores, axis=1, keepdims=True), jnp.max(late, axis=1, keepdims=True))
            scores = jnp.exp(scores - top)
            late = jnp.exp(late - top)
            rate = 1.0 / (jnp.sum(scores, axis=1, keepdims=True) + jnp.sum(late, axis=1, keepdims=True))
            scores = (scores * rate).astype(jnp.bfloat16)
            late = (late * rate).astype(jnp.bfloat16)
            out = mine(
                [jnp.dot(scores, old[b, 1], preferred_element_type=jnp.float32) for b in members], line
            )
            out = out + jnp.dot(late, fresh[1], preferred_element_type=jnp.float32)
            rest = mine([jnp.full((many, HD), left[b], jnp.int32) for b in members], line)
            out = jnp.where(line % steps < rest, out, 0.0)
            for h in range(heads):
                mixed[p * 8 : (p + 1) * 8, h * HD : (h + 1) * HD] = out[h * 8 : (h + 1) * 8]

        done_rows = mixed[...].astype(jnp.bfloat16)
        rows_ref[...] = done_rows
        column = lax.broadcasted_iota(jnp.int32, (sends, rows), 1)
        upper = lax.broadcasted_iota(jnp.int32, (sends, rows), 0) % TILE < TILE // 2
        chosen = pick_ref[...] == column
        first = jnp.where(chosen & upper, 1.0, 0.0).astype(jnp.bfloat16)
        second = jnp.where(chosen & jnp.logical_not(upper), 1.0, 0.0).astype(jnp.bfloat16)
        for c in range(chunks // 2):
            lanes = slice(2 * c * HD, (2 * c + 1) * HD)
            after = slice((2 * c + 1) * HD, (2 * c + 2) * HD)
            tile = jnp.dot(first, done_rows[:, lanes], preferred_element_type=jnp.float32) + jnp.dot(
                second, done_rows[:, after], preferred_element_type=jnp.float32
            )
            send_ref[c] = tile.astype(jnp.bfloat16)

    vmem = pl.BlockSpec(memory_space=pltpu.VMEM)
    smem = pl.BlockSpec(memory_space=pltpu.SMEM)
    hbm = pl.BlockSpec(memory_space=pltpu.HBM)
    return pl.pallas_call(
        kernel,
        in_specs=[smem] * 4 + [vmem] * count + [vmem, hbm, hbm] + [vmem] * 5 + [hbm],
        out_specs=[vmem, vmem],
        scratch_shapes=[
            pltpu.VMEM((model_width, width), jnp.bfloat16),
            pltpu.VMEM((2, model_width, HD), jnp.bfloat16),
            pltpu.VMEM((rows, wide), jnp.float32),
            pltpu.VMEM((slots, 2, span, HD), jnp.bfloat16),
            pltpu.VMEM((rows * heads, HD), jnp.float32),
            pltpu.VMEM((2, HD, HD), jnp.bfloat16),
            pltpu.VMEM((rows, wide), jnp.float32),
            pltpu.SemaphoreType.DMA((2 * count,)),
            pltpu.SemaphoreType.DMA((slots,)),
        ],
        out_shape=[
            jax.ShapeDtypeStruct((rows, wide), jnp.bfloat16),
            jax.ShapeDtypeStruct((chunks // 2, sends, HD), jnp.bfloat16),
        ],
        compiler_params=pltpu.CompilerParams(vmem_limit_bytes=57 * 1024 * 1024),
        cost_estimate=pl.CostEstimate(flops=2 * rows * wide, bytes_accessed=rows * wide, transcendentals=0),
        name="project_attend",
    )(
        page_table.reshape(-1), context, remaining, origin, *parts, gain.reshape(count, 1, depth), w_query, w_keyval,
        b_query.reshape(1, width), b_keyval, cos, sin, pick.reshape(sends, 1), cache,
    )


def gather_parts(rows):
    count = lax.axis_size("tensor")
    here = lax.axis_index("tensor").astype(jnp.int32)
    chips = count // 2
    shifts = [k for k in (1, chips - 1, *range(2, chips - 1)) if k < chips]
    shifts = list(dict.fromkeys(shifts))
    near = [rows]
    for k in shifts:
        near.append(lax.ppermute(rows, "tensor", [(r, (r + 2 * k) % count) for r in range(count)]))
    far = [lax.ppermute(part, "tensor", [(r, r ^ 1) for r in range(count)]) for part in near]
    back = jnp.array([0] + [2 * k for k in shifts], jnp.int32)
    origin = (here - back) % count
    return near + far, jnp.concatenate([origin, origin ^ 1])


def settle(landed, mine, take, pages, width):
    ranks, tiles = landed.shape[:2]
    rows, wide = mine.shape
    chunks = wide // HD
    span = (tiles - chunks // 2) // ARR
    part = span // 2
    slots = rows // STEPS

    def kernel(landed_ref, mine_ref, take_ref, out_ref, kv_ref, arrived_ref, sems):
        copies = [
            pltpu.make_async_copy(
                landed_ref.at[:, pl.ds(a * span + kind * part, part)], arrived_ref.at[kind, a], sems.at[2 * a + kind]
            )
            for a in range(ARR)
            for kind in range(2)
        ]
        for copy in copies:
            copy.start()
        index = take_ref[:, :1]
        own = (index == lax.broadcasted_iota(jnp.int32, (rows, rows), 1)).astype(jnp.bfloat16)
        place = lax.broadcasted_iota(jnp.int32, (rows, ranks * TILE), 1)
        half = TILE // 2
        flat = rows + place // TILE * half + place % half
        upper = place % TILE < half
        hit = index == flat
        came = [
            jnp.where(hit & upper, 1.0, 0.0).astype(jnp.bfloat16),
            jnp.where(hit & jnp.logical_not(upper), 1.0, 0.0).astype(jnp.bfloat16),
        ]
        for c in range(chunks):
            lanes = slice(c * HD, (c + 1) * HD)
            got = landed_ref[:, ARR * span + c // 2].reshape(ranks * TILE, HD)
            final = jnp.dot(own, mine_ref[:, lanes], preferred_element_type=jnp.float32) + jnp.dot(
                came[c % 2], got, preferred_element_type=jnp.float32
            )
            final = final.reshape(slots, STEPS, HD).astype(jnp.bfloat16)
            if c < chunks - 2:
                out_ref[:, :, lanes] = final
            else:
                kv_ref[c - (chunks - 2)] = final
        for copy in copies:
            copy.wait()

    vmem = pl.BlockSpec(memory_space=pltpu.VMEM)
    return pl.pallas_call(
        kernel,
        in_specs=[vmem] * 3,
        out_specs=[vmem, vmem, pl.BlockSpec(memory_space=pltpu.HBM)],
        scratch_shapes=[pltpu.SemaphoreType.DMA((2 * ARR,))],
        out_shape=[
            jax.ShapeDtypeStruct((slots, STEPS, width), jnp.bfloat16),
            jax.ShapeDtypeStruct((2, slots, STEPS, HD), jnp.bfloat16),
            jax.ShapeDtypeStruct((2, ARR, ranks, part, TILE, HD), jnp.bfloat16),
        ],
        compiler_params=pltpu.CompilerParams(vmem_limit_bytes=16 * 1024 * 1024),
        name="settle",
    )(landed, mine, take)


def local(
    hidden, norm_gain, w_query, w_keyval, b_query, b_keyval, cache, page_table, context, remaining, move_to
):
    slots, steps, depth = hidden.shape
    ranks = lax.axis_size("dp")
    rank = lax.axis_index("dp").astype(jnp.int32)
    page = cache.shape[2]
    pages = page_table.shape[1]
    width = w_query.shape[1]
    rows = slots * steps
    ids = jnp.arange(slots, dtype=jnp.int32)

    sent = pack_pages(page_table, context, remaining, move_to, cache, ranks)
    sent, hidden = lax.optimization_barrier((sent, hidden))
    received = lax.all_to_all(sent, "dp", 0, 0, tiled=True)

    staying = move_to == ids + rank * slots
    leaving = jnp.logical_not(staying) & (remaining > 0)
    coming = jnp.logical_not(staying) & (remaining == 0)
    there = move_to // slots
    same = there[None, :] == there[:, None]
    leave_order = jnp.sum((same & leaving[None, :] & (ids[None, :] < ids[:, None])).astype(jnp.int32), axis=1)
    come_order = jnp.sum(
        (same & coming[None, :] & (move_to[None, :] < move_to[:, None])).astype(jnp.int32), axis=1
    )
    place = jnp.where(leaving, there * CAP + leave_order, -1)
    hit = place[None, :] == jnp.arange(ranks * CAP, dtype=jnp.int32)[:, None]
    slot_of = jnp.max(jnp.where(hit, ids[None, :], -1), axis=1)
    step_ids = jnp.arange(steps, dtype=jnp.int32)
    pick = jnp.where(slot_of[:, None] >= 0, slot_of[:, None] * steps + step_ids[None, :], -1)
    pick = jnp.broadcast_to(pick.reshape(ranks, 1, CAP * steps), (ranks, 2, CAP * steps)).reshape(-1)

    half = HD // 2
    inverse = rope_base ** (-(jnp.arange(half, dtype=jnp.float32) * (2.0 / HD)))
    positions = (context[:, None] + step_ids[None, :]).reshape(-1).astype(jnp.float32)
    angles = positions[:, None] * inverse[None, :]
    cos, sin = jnp.cos(angles), jnp.sin(angles)
    cos = jnp.concatenate([cos, cos], axis=1)
    sin = jnp.concatenate([-sin, sin], axis=1)

    parts, origin = gather_parts(hidden.reshape(rows, depth))
    mine, going = project_attend(
        page_table, context, remaining, origin, parts, norm_gain, w_query, w_keyval, b_query, b_keyval, cos, sin,
        pick, cache,
    )
    base = jnp.where(staying, ids * steps, jnp.where(coming, rows + (there * CAP + come_order) * steps, -steps))
    take = (base[:, None] + step_ids[None, :]).reshape(-1, 1)
    received, mine, going, take = lax.optimization_barrier((received, mine, going, take))
    goals = received[:, -1, 0, :ARR].astype(jnp.int32).reshape(-1)
    relayed, take = relay_pages(plan_relay(goals, slots, ranks), received, going, take)
    landed = lax.all_to_all(relayed, "dp", 0, 0, tiled=True)
    attended, new_keyval, arrived = settle(landed, mine, take, pages, width)
    return attended, new_keyval, arrived.reshape(2, ARR, pages * page, HD)


def solution(mesh):
    in_specs = (
        P("dp", None, "tensor"),
        P(),
        P(None, "tensor"),
        P(None, None, "tensor"),
        P("tensor"),
        P(None, "tensor"),
        P(None, "dp", None, "tensor"),
        P("dp", None),
        P("dp"),
        P("dp"),
        P("dp"),
    )
    out_specs = (
        P("dp", None, "tensor"),
        P(None, "dp", None, "tensor"),
        P(None, "dp", None, "tensor"),
    )
    return jax.shard_map(local, mesh=mesh, in_specs=in_specs, out_specs=out_specs, check_vma=False)
```

```python
import math

import jax
import jax.numpy as jnp
from jax import lax
from jax.experimental import pallas as pl
from jax.experimental.pallas import tpu as pltpu
from jax.sharding import PartitionSpec as P

HD = 128
ARR = 4
CAP = 2
TILE = 16
STEPS = 4

rope_base = 1000000.0
norm_eps = 1e-06
masked_score = -1e30


def pack_pages(page_table, context, remaining, move_to, cache, ranks):
    slots, pages = page_table.shape
    page = cache.shape[2]
    tiles = page // TILE
    pool = cache.reshape(2, cache.shape[1], tiles, TILE, HD)
    last = ARR * 2 * tiles

    def kernel(
        table_hbm, ctx_hbm, left_hbm, goal_hbm, pool_ref, out_ref, table, ctx, left, goal, list_ref, stage, sems, small,
    ):
        reads = [
            pltpu.make_async_copy(src, dst, small.at[n])
            for n, (src, dst) in enumerate(
                ((table_hbm, table), (ctx_hbm, ctx), (left_hbm, left), (goal_hbm, goal))
            )
        ]
        for read in reads:
            read.start()
        for read in reads:
            read.wait()
        first = lax.axis_index("dp").astype(jnp.int32) * slots

        for m in range(ARR):
            list_ref[m] = 0
        count = jnp.int32(0)
        for b in range(slots):
            leaves = jnp.logical_and(left[b] > 0, goal[b] != first + b)
            list_ref[jnp.where(leaves, jnp.minimum(count, ARR - 1), ARR)] = b
            count = count + leaves.astype(jnp.int32)
        count = jnp.minimum(count, ARR)

        def used(m):
            return lax.div(ctx[list_ref[m]] + page - 1, page)

        def reads_of(m, j):
            b = list_ref[m]
            return [
                pltpu.make_async_copy(
                    pool_ref.at[kind, table[b, j]], stage.at[j, pl.ds((m * 2 + kind) * tiles, tiles)], sems.at[m]
                )
                for kind in range(2)
            ]

        def start(m, carry):
            def one(j, inner):
                for copy in reads_of(m, j):
                    copy.start()
                return inner

            return lax.fori_loop(0, used(m), one, carry)

        lax.fori_loop(0, count, start, 0)
        lane = lax.broadcasted_iota(jnp.int32, (TILE, HD), 1)
        note_tile = jnp.full((TILE, HD), 512, jnp.int32)
        for m in range(ARR):
            note_tile = jnp.where(lane == m, jnp.where(m < count, goal[list_ref[m]], 512), note_tile)
        note_tile = note_tile.astype(jnp.float32).astype(jnp.bfloat16)
        for j in range(ranks):
            stage[j, last] = note_tile
        notes = pltpu.make_async_copy(
            stage.at[:, pl.ds(last, 1)], out_ref.at[:, pl.ds(last, 1)], sems.at[ARR + 1]
        )
        notes.start()

        def write_of(m):
            at = pl.ds(m * 2 * tiles, 2 * tiles)
            return pltpu.make_async_copy(stage.at[:, at], out_ref.at[:, at], sems.at[ARR])

        def clear(m, carry):
            def one(j, inner):
                stage[j, pl.ds(m * 2 * tiles, 2 * tiles)] = jnp.zeros((2 * tiles, TILE, HD), jnp.bfloat16)
                return inner

            return lax.fori_loop(used(m), pages, one, carry)

        lax.fori_loop(0, count, clear, 0)
        row = lax.broadcasted_iota(jnp.int32, (tiles, TILE, HD), 0) * TILE + lax.broadcasted_iota(
            jnp.int32, (tiles, TILE, HD), 1
        )

        def finish(m, carry):
            full = used(m)

            def one(j, inner):
                for copy in reads_of(m, j):
                    copy.wait()
                return inner

            lax.fori_loop(0, full, one, 0)
            rest = ctx[list_ref[m]] - (full - 1) * page
            for kind in range(2):
                at = pl.ds((m * 2 + kind) * tiles, tiles)
                edge = stage[full - 1, at]
                stage[full - 1, at] = jnp.where(row < rest, edge, jnp.zeros_like(edge))
            write_of(m).start()
            return carry

        def settle_writes(m, carry):
            write_of(m).wait()
            return carry

        lax.fori_loop(0, count, finish, 0)
        lax.fori_loop(0, count, settle_writes, 0)
        notes.wait()

    hbm = pl.BlockSpec(memory_space=pltpu.HBM)
    return pl.pallas_call(
        kernel,
        in_specs=[hbm] * 5,
        out_specs=hbm,
        scratch_shapes=[
            pltpu.SMEM((slots, pages), jnp.int32),
            pltpu.SMEM((slots,), jnp.int32),
            pltpu.SMEM((slots,), jnp.int32),
            pltpu.SMEM((slots,), jnp.int32),
            pltpu.SMEM((ARR + 1,), jnp.int32),
            pltpu.VMEM((ranks, last + 1, TILE, HD), jnp.bfloat16),
            pltpu.SemaphoreType.DMA((ARR + 2,)),
            pltpu.SemaphoreType.DMA((4,)),
        ],
        out_shape=jax.ShapeDtypeStruct((ranks, last + 1, TILE, HD), jnp.bfloat16),
        compiler_params=pltpu.CompilerParams(vmem_limit_bytes=56 * 1024 * 1024),
        name="pack_pages",
    )(page_table, context, remaining, move_to, pool)


def relay_pages(source, received, going):
    ranks, rows = received.shape[:2]
    span = (rows - 1) // ARR
    more = going.shape[0]

    def kernel(src, got_ref, going_ref, out_ref):
        for d in range(ranks):
            for a in range(ARR):
                k = src[d * ARR + a]
                place = jnp.maximum(k, 0)
                block = got_ref[place // ARR, pl.ds((place & (ARR - 1)) * span, span)]
                out_ref[d, a * span : (a + 1) * span] = jnp.where(k >= 0, block, jnp.zeros_like(block))
            for c in range(more):
                out_ref[d, ARR * span + c] = going_ref[c, d * TILE : (d + 1) * TILE]

    vmem = pl.BlockSpec(memory_space=pltpu.VMEM)
    return pl.pallas_call(
        kernel,
        in_specs=[pl.BlockSpec(memory_space=pltpu.SMEM), vmem, vmem],
        out_specs=vmem,
        out_shape=jax.ShapeDtypeStruct((ranks, ARR * span + more, TILE, HD), jnp.bfloat16),
        compiler_params=pltpu.CompilerParams(vmem_limit_bytes=16 * 1024 * 1024),
        name="relay_pages",
    )(source, received, going)


def plan_relay(goals, slots, ranks):
    count = goals.shape[0]
    home = goals // slots
    before = (home[None, :] == home[:, None]) & (goals[None, :] < goals[:, None])
    order = jnp.sum(before.astype(jnp.int32), axis=1)
    target = home * ARR + order
    ids = jnp.arange(count, dtype=jnp.int32)
    hit = target[None, :] == jnp.arange(ranks * ARR, dtype=jnp.int32)[:, None]
    return jnp.max(jnp.where(hit, ids[None, :], -1), axis=1)


def into_vmem(array, pieces, name):
    size = array.shape[0] // pieces

    def kernel(in_ref, out_ref, sems):
        copies = [
            pltpu.make_async_copy(
                in_ref.at[pl.ds(n * size, size)], out_ref.at[pl.ds(n * size, size)], sems.at[n]
            )
            for n in range(pieces)
        ]
        for copy in copies:
            copy.start()
        for copy in copies:
            copy.wait()

    return pl.pallas_call(
        kernel,
        in_specs=[pl.BlockSpec(memory_space=pltpu.HBM)],
        out_specs=pl.BlockSpec(memory_space=pltpu.VMEM),
        scratch_shapes=[pltpu.SemaphoreType.DMA((pieces,))],
        out_shape=jax.ShapeDtypeStruct(array.shape, array.dtype),
        compiler_params=pltpu.CompilerParams(vmem_limit_bytes=16 * 1024 * 1024),
        cost_estimate=pl.CostEstimate(flops=0, bytes_accessed=2 * array.size * 2, transcendentals=0),
        name=name,
    )(array)


def old_pages(page_table, context, remaining, w_keyval, cache):
    slots, pages = page_table.shape
    page = cache.shape[2]

    def kernel(table, ctx, left, w_ref, cache_ref, old, w_out, sems, sem):
        weights = pltpu.make_async_copy(w_ref, w_out, sem)
        weights.start()

        def used(b):
            return jnp.where(left[b] > 0, lax.div(ctx[b] + page - 1, page), 0)

        def copy_page(b, j):
            return pltpu.make_async_copy(
                cache_ref.at[:, table[b, j]], old.at[b, :, pl.ds(j * page, page)], sems.at[b]
            )

        def fetch(b, carry):
            def one(j, inner):
                copy_page(b, j).start()
                return inner

            def clear(j, inner):
                old[b, 1, pl.ds(j * page, page)] = jnp.zeros((page, HD), jnp.bfloat16)
                return inner

            lax.fori_loop(0, used(b), one, 0)
            return lax.fori_loop(used(b), pages, clear, carry)

        def finish(b, carry):
            def one(j, inner):
                copy_page(b, j).wait()
                return inner

            return lax.fori_loop(0, used(b), one, carry)

        lax.fori_loop(0, slots, fetch, 0)
        lax.fori_loop(0, slots, finish, 0)
        weights.wait()

    smem = pl.BlockSpec(memory_space=pltpu.SMEM)
    hbm = pl.BlockSpec(memory_space=pltpu.HBM)
    vmem = pl.BlockSpec(memory_space=pltpu.VMEM)
    return pl.pallas_call(
        kernel,
        in_specs=[smem] * 3 + [hbm] * 2,
        out_specs=[vmem, vmem],
        scratch_shapes=[pltpu.SemaphoreType.DMA((slots,)), pltpu.SemaphoreType.DMA(())],
        out_shape=[
            jax.ShapeDtypeStruct((slots, 2, pages * page, HD), cache.dtype),
            jax.ShapeDtypeStruct(w_keyval.shape, w_keyval.dtype),
        ],
        compiler_params=pltpu.CompilerParams(vmem_limit_bytes=27 * 1024 * 1024),
        cost_estimate=pl.CostEstimate(flops=0, bytes_accessed=24 * 1024 * 1024, transcendentals=0),
        name="old_pages",
    )(page_table, context, remaining, w_keyval, cache)


def project_attend(context, remaining, origin, parts, gain, w_query, w_keyval, b_query, b_keyval, cos, sin, pick, old):
    slots, span = old.shape[0], old.shape[2]
    count = len(parts)
    rows, depth = parts[0].shape
    steps = rows // slots
    width = w_query.shape[1]
    wide = width + 2 * HD
    heads = width // HD
    sends = pick.shape[1]
    chunks = wide // HD
    pair = 8 // steps
    scale = 1.0 / math.sqrt(HD)
    model_width = count * depth

    def kernel(*refs):
        ctx, left, source = refs[:3]
        hid = refs[3 : 3 + count]
        (
            gain_ref, wq, wkv, bq_ref, bkv_ref, cos_ref, sin_ref, pick_ref, old,
            rows_ref, send_ref, acc, query, fresh, mixed,
        ) = refs[3 + count :]

        squares = jnp.zeros((rows, 1), jnp.float32)
        for i in range(count):
            part = hid[i][...].astype(jnp.float32)
            normed = (part * gain_ref[source[i]].astype(jnp.float32)).astype(jnp.bfloat16)
            squares += jnp.sum(part * part, axis=1, keepdims=True)
            at = pl.ds(pl.multiple_of(source[i] * depth, depth), depth)
            sums = [
                jnp.dot(normed, wq[at], preferred_element_type=jnp.float32),
                jnp.dot(normed, wkv[0, at], preferred_element_type=jnp.float32),
                jnp.dot(normed, wkv[1, at], preferred_element_type=jnp.float32),
            ]
            for lanes, part_sum in zip(
                (slice(0, width), slice(width, width + HD), slice(width + HD, wide)), sums, strict=True
            ):
                if i:
                    acc[:, lanes] += part_sum
                else:
                    acc[:, lanes] = part_sum

        row_scale = lax.rsqrt(squares / model_width + norm_eps)
        cosine, sine = cos_ref[...], sin_ref[...]

        def rotate(x):
            return x * cosine + pltpu.roll(x, HD // 2, 1) * sine

        many = heads * 8
        for h in range(heads):
            at = slice(h * HD, (h + 1) * HD)
            q = rotate(acc[:, at] * row_scale + bq_ref[:, at].astype(jnp.float32))
            for p in range(rows // 8):
                query[p * many + h * 8 : p * many + (h + 1) * 8, :] = q[p * 8 : (p + 1) * 8, :]
        key = rotate(acc[:, width : width + HD] * row_scale + bkv_ref[0:1].astype(jnp.float32))
        value = acc[:, width + HD :] * row_scale + bkv_ref[1:2].astype(jnp.float32)
        fresh[0, :rows] = key.astype(jnp.bfloat16)
        fresh[1, :rows] = value.astype(jnp.bfloat16)
        fresh[:, rows:] = jnp.zeros((2, HD - rows, HD), jnp.bfloat16)
        row_of = lax.broadcasted_iota(jnp.int32, (rows, HD), 0)
        live_of = jnp.zeros((rows, HD), jnp.int32)
        for b in range(slots):
            live_of = jnp.where(row_of // steps == b, left[b], live_of)
        alive = row_of % steps < live_of
        mixed[:, width : width + HD] = jnp.where(alive, key, 0.0)
        mixed[:, width + HD :] = jnp.where(alive, value, 0.0)

        col = lax.broadcasted_iota(jnp.int32, (many, span), 1)
        new_col = lax.broadcasted_iota(jnp.int32, (many, HD), 1)
        line = lax.broadcasted_iota(jnp.int32, (many, HD), 0) % 8
        line_one = lax.broadcasted_iota(jnp.int32, (many, 1), 0) % 8
        for p in range(slots // pair):
            members = range(p * pair, (p + 1) * pair)
            q = query[p * many : (p + 1) * many, :].astype(jnp.bfloat16)

            def mine(values, at):
                out = values[0]
                for n in range(1, pair):
                    out = jnp.where(at >= n * steps, values[n], out)
                return out

            wide_line = jnp.broadcast_to(line_one, (many, span))
            scores = mine(
                [
                    lax.dot_general(q, old[b, 0], (((1,), (1,)), ((), ())), preferred_element_type=jnp.float32)
                    for b in members
                ],
                wide_line,
            )
            limit = mine([jnp.full((many, 1), ctx[b], jnp.int32) for b in members], line_one)
            scores = jnp.where(col < limit, scores * scale, masked_score)
            late = lax.dot_general(q, fresh[0], (((1,), (1,)), ((), ())), preferred_element_type=jnp.float32)
            since = new_col - p * 8
            seen = (since >= (line // steps) * steps) & (since <= line)
            late = jnp.where(seen, late * scale, masked_score)
            top = jnp.maximum(jnp.max(scores, axis=1, keepdims=True), jnp.max(late, axis=1, keepdims=True))
            scores = jnp.exp(scores - top)
            late = jnp.exp(late - top)
            rate = 1.0 / (jnp.sum(scores, axis=1, keepdims=True) + jnp.sum(late, axis=1, keepdims=True))
            scores = (scores * rate).astype(jnp.bfloat16)
            late = (late * rate).astype(jnp.bfloat16)
            out = mine(
                [jnp.dot(scores, old[b, 1], preferred_element_type=jnp.float32) for b in members], line
            )
            out = out + jnp.dot(late, fresh[1], preferred_element_type=jnp.float32)
            rest = mine([jnp.full((many, HD), left[b], jnp.int32) for b in members], line)
            out = jnp.where(line % steps < rest, out, 0.0)
            for h in range(heads):
                mixed[p * 8 : (p + 1) * 8, h * HD : (h + 1) * HD] = out[h * 8 : (h + 1) * 8]

        done_rows = mixed[...].astype(jnp.bfloat16)
        rows_ref[...] = done_rows
        column = lax.broadcasted_iota(jnp.int32, (rows, sends), 0)
        upper = lax.broadcasted_iota(jnp.int32, (rows, sends), 1) % TILE < TILE // 2
        chosen = pick_ref[...] == column
        first = jnp.where(chosen & upper, 1.0, 0.0).astype(jnp.bfloat16)
        second = jnp.where(chosen & jnp.logical_not(upper), 1.0, 0.0).astype(jnp.bfloat16)
        down = (((0,), (0,)), ((), ()))
        for c in range(chunks // 2):
            lanes = slice(2 * c * HD, (2 * c + 1) * HD)
            after = slice((2 * c + 1) * HD, (2 * c + 2) * HD)
            tile = lax.dot_general(
                first, done_rows[:, lanes], down, preferred_element_type=jnp.float32
            ) + lax.dot_general(second, done_rows[:, after], down, preferred_element_type=jnp.float32)
            send_ref[c] = tile.astype(jnp.bfloat16)

    vmem = pl.BlockSpec(memory_space=pltpu.VMEM)
    smem = pl.BlockSpec(memory_space=pltpu.SMEM)
    return pl.pallas_call(
        kernel,
        in_specs=[smem] * 3 + [vmem] * (count + 9),
        out_specs=[vmem, vmem],
        scratch_shapes=[
            pltpu.VMEM((rows, wide), jnp.float32),
            pltpu.VMEM((rows * heads, HD), jnp.float32),
            pltpu.VMEM((2, HD, HD), jnp.bfloat16),
            pltpu.VMEM((rows, wide), jnp.float32),
        ],
        out_shape=[
            jax.ShapeDtypeStruct((rows, wide), jnp.bfloat16),
            jax.ShapeDtypeStruct((chunks // 2, sends, HD), jnp.bfloat16),
        ],
        compiler_params=pltpu.CompilerParams(vmem_limit_bytes=16 * 1024 * 1024),
        cost_estimate=pl.CostEstimate(
            flops=2 * rows * model_width * wide, bytes_accessed=32 * 1024 * 1024, transcendentals=rows * heads * span
        ),
        name="project_attend",
    )(context, remaining, origin, *parts, gain, w_query, w_keyval, b_query, b_keyval, cos, sin, pick, old)


def from_chips(rows):
    count = lax.axis_size("tensor")
    here = lax.axis_index("tensor").astype(jnp.int32)
    chips = count // 2
    shifts = [0] + list(dict.fromkeys(k for k in (1, chips - 1, *range(2, chips)) if 0 < k < chips))
    parts = [lax.ppermute(rows, "tensor", [(r, (r + 2 * k) % count) for r in range(count)]) if k else rows for k in shifts]
    origin = (here - jnp.array([2 * k for k in shifts], jnp.int32)) % count
    return parts, jnp.concatenate([origin, origin ^ 1])


def from_sibling(parts):
    count = lax.axis_size("tensor")
    return [lax.ppermute(part, "tensor", [(r, r ^ 1) for r in range(count)]) for part in parts]


def settle(landed, mine, take, pages, width):
    ranks, tiles = landed.shape[:2]
    rows, wide = mine.shape
    chunks = wide // HD
    span = (tiles - chunks // 2) // ARR
    part = span // 2
    slots = rows // STEPS

    def kernel(landed_ref, mine_ref, take_ref, out_ref, kv_ref, arrived_ref, sems):
        copies = [
            pltpu.make_async_copy(
                landed_ref.at[:, pl.ds(a * span + kind * part, part)], arrived_ref.at[kind, a], sems.at[2 * a + kind]
            )
            for a in range(ARR)
            for kind in range(2)
        ]
        for copy in copies:
            copy.start()
        index = take_ref[...]
        own = (index == lax.broadcasted_iota(jnp.int32, (rows, rows), 0)).astype(jnp.bfloat16)
        place = lax.broadcasted_iota(jnp.int32, (ranks * TILE, rows), 0)
        half = TILE // 2
        flat = rows + place // TILE * half + place % half
        upper = place % TILE < half
        hit = index == flat
        came = [
            jnp.where(hit & upper, 1.0, 0.0).astype(jnp.bfloat16),
            jnp.where(hit & jnp.logical_not(upper), 1.0, 0.0).astype(jnp.bfloat16),
        ]
        down = (((0,), (0,)), ((), ()))
        for c in range(chunks):
            lanes = slice(c * HD, (c + 1) * HD)
            got = landed_ref[:, ARR * span + c // 2].reshape(ranks * TILE, HD)
            final = lax.dot_general(
                own, mine_ref[:, lanes], down, preferred_element_type=jnp.float32
            ) + lax.dot_general(came[c % 2], got, down, preferred_element_type=jnp.float32)
            final = final.reshape(slots, STEPS, HD).astype(jnp.bfloat16)
            if c < chunks - 2:
                out_ref[:, :, lanes] = final
            else:
                kv_ref[c - (chunks - 2)] = final
        for copy in copies:
            copy.wait()

    vmem = pl.BlockSpec(memory_space=pltpu.VMEM)
    return pl.pallas_call(
        kernel,
        in_specs=[vmem] * 3,
        out_specs=[vmem, vmem, pl.BlockSpec(memory_space=pltpu.HBM)],
        scratch_shapes=[pltpu.SemaphoreType.DMA((2 * ARR,))],
        out_shape=[
            jax.ShapeDtypeStruct((slots, STEPS, width), jnp.bfloat16),
            jax.ShapeDtypeStruct((2, slots, STEPS, HD), jnp.bfloat16),
            jax.ShapeDtypeStruct((2, ARR, ranks, part, TILE, HD), jnp.bfloat16),
        ],
        compiler_params=pltpu.CompilerParams(vmem_limit_bytes=16 * 1024 * 1024),
        name="settle",
    )(landed, mine, take)


def local(
    hidden, norm_gain, w_query, w_keyval, b_query, b_keyval, cache, page_table, context, remaining, move_to
):
    slots, steps, depth = hidden.shape
    ranks = lax.axis_size("dp")
    rank = lax.axis_index("dp").astype(jnp.int32)
    page = cache.shape[2]
    pages = page_table.shape[1]
    width = w_query.shape[1]
    rows = slots * steps
    ids = jnp.arange(slots, dtype=jnp.int32)

    sent = pack_pages(page_table, context, remaining, move_to, cache, ranks)
    sent, hidden = lax.optimization_barrier((sent, hidden))
    received = lax.all_to_all(sent, "dp", 0, 0, tiled=True)

    staying = move_to == ids + rank * slots
    leaving = jnp.logical_not(staying) & (remaining > 0)
    coming = jnp.logical_not(staying) & (remaining == 0)
    there = move_to // slots
    same = there[None, :] == there[:, None]
    leave_order = jnp.sum((same & leaving[None, :] & (ids[None, :] < ids[:, None])).astype(jnp.int32), axis=1)
    come_order = jnp.sum(
        (same & coming[None, :] & (move_to[None, :] < move_to[:, None])).astype(jnp.int32), axis=1
    )
    place = jnp.where(leaving, there * CAP + leave_order, -1)
    hit = place[None, :] == jnp.arange(ranks * CAP, dtype=jnp.int32)[:, None]
    slot_of = jnp.max(jnp.where(hit, ids[None, :], -1), axis=1)
    step_ids = jnp.arange(steps, dtype=jnp.int32)
    pick = jnp.where(slot_of[:, None] >= 0, slot_of[:, None] * steps + step_ids[None, :], -1)
    pick = jnp.broadcast_to(pick.reshape(ranks, 1, CAP * steps), (ranks, 2, CAP * steps)).reshape(1, -1)

    half = HD // 2
    inverse = rope_base ** (-(jnp.arange(half, dtype=jnp.float32) * (2.0 / HD)))
    positions = (context[:, None] + step_ids[None, :]).reshape(-1).astype(jnp.float32)
    angles = positions[:, None] * inverse[None, :]
    cos, sin = jnp.cos(angles), jnp.sin(angles)
    cos = jnp.concatenate([cos, cos], axis=1)
    sin = jnp.concatenate([-sin, sin], axis=1)

    def attend(hidden):
        near, origin = from_chips(hidden.reshape(rows, depth))
        weights = into_vmem(w_query, 16, "query_weights")
        small = (
            origin, norm_gain.reshape(-1, 1, depth), b_query.reshape(1, width), b_keyval, cos, sin, pick, page_table,
            context, remaining,
        )
        near, weights, small = lax.optimization_barrier((near, weights, small))
        origin, gain, bias, bias_keyval, cosine, sine, picked, table, tokens, left = small
        far = from_sibling(near)
        old, weights_keyval = old_pages(table, tokens, left, w_keyval, cache)
        return tuple(
            project_attend(
                tokens, left, origin, near + far, gain, weights, weights_keyval, bias, bias_keyval, cosine, sine,
                picked, old,
            )
        )

    def nothing(hidden):
        wide = width + 2 * HD
        return jnp.zeros((rows, wide), jnp.bfloat16), jnp.zeros((wide // HD // 2, pick.shape[1], HD), jnp.bfloat16)

    mine, going = lax.cond(context[0] > 0, attend, nothing, hidden)
    base = jnp.where(staying, ids * steps, jnp.where(coming, rows + (there * CAP + come_order) * steps, -steps))
    take = (base[:, None] + step_ids[None, :]).reshape(1, -1)
    received, mine, going, take = lax.optimization_barrier((received, mine, going, take))
    goals = received[:, -1, 0, :ARR].astype(jnp.int32).reshape(-1)
    relayed = relay_pages(plan_relay(goals, slots, ranks), received, going)
    landed = lax.all_to_all(relayed, "dp", 0, 0, tiled=True)
    attended, new_keyval, arrived = settle(landed, mine, take, pages, width)
    return attended, new_keyval, arrived.reshape(2, ARR, pages * page, HD)


def solution(mesh):
    in_specs = (
        P("dp", None, "tensor"),
        P(),
        P(None, "tensor"),
        P(None, None, "tensor"),
        P("tensor"),
        P(None, "tensor"),
        P(None, "dp", None, "tensor"),
        P("dp", None),
        P("dp"),
        P("dp"),
        P("dp"),
    )
    out_specs = (
        P("dp", None, "tensor"),
        P(None, "dp", None, "tensor"),
        P(None, "dp", None, "tensor"),
    )
    return jax.shard_map(local, mesh=mesh, in_specs=in_specs, out_specs=out_specs, check_vma=False)
```

```python
import math

import jax
import jax.numpy as jnp
from jax import lax
from jax.experimental import pallas as pl
from jax.experimental.pallas import tpu as pltpu
from jax.sharding import PartitionSpec as P

HD = 128
ARR = 4
CAP = 2
TILE = 16
STEPS = 4

rope_base = 1000000.0
norm_eps = 1e-06
masked_score = -1e30


def pack_pages(page_table, context, remaining, move_to, cache, ranks):
    slots, pages = page_table.shape
    page = cache.shape[2]
    tiles = page // TILE
    pool = cache.reshape(2, cache.shape[1], tiles, TILE, HD)
    last = ARR * 2 * tiles

    def kernel(
        table_hbm, ctx_hbm, left_hbm, goal_hbm, pool_ref, out_ref, table, ctx, left, goal, list_ref, stage, sems, small,
    ):
        reads = [
            pltpu.make_async_copy(src, dst, small.at[n])
            for n, (src, dst) in enumerate(
                ((table_hbm, table), (ctx_hbm, ctx), (left_hbm, left), (goal_hbm, goal))
            )
        ]
        for read in reads:
            read.start()
        for read in reads:
            read.wait()
        first = lax.axis_index("dp").astype(jnp.int32) * slots

        for m in range(ARR):
            list_ref[m] = 0
        count = jnp.int32(0)
        for b in range(slots):
            leaves = jnp.logical_and(left[b] > 0, goal[b] != first + b)
            list_ref[jnp.where(leaves, jnp.minimum(count, ARR - 1), ARR)] = b
            count = count + leaves.astype(jnp.int32)
        count = jnp.minimum(count, ARR)

        def used(m):
            return lax.div(ctx[list_ref[m]] + page - 1, page)

        def reads_of(m, j):
            b = list_ref[m]
            return [
                pltpu.make_async_copy(
                    pool_ref.at[kind, table[b, j]], stage.at[j, pl.ds((m * 2 + kind) * tiles, tiles)], sems.at[m]
                )
                for kind in range(2)
            ]

        def start(m, carry):
            def one(j, inner):
                for copy in reads_of(m, j):
                    copy.start()
                return inner

            return lax.fori_loop(0, used(m), one, carry)

        lax.fori_loop(0, count, start, 0)
        lane = lax.broadcasted_iota(jnp.int32, (TILE, HD), 1)
        note_tile = jnp.full((TILE, HD), 512, jnp.int32)
        for m in range(ARR):
            note_tile = jnp.where(lane == m, jnp.where(m < count, goal[list_ref[m]], 512), note_tile)
        note_tile = note_tile.astype(jnp.float32).astype(jnp.bfloat16)
        for j in range(ranks):
            stage[j, last] = note_tile
        notes = pltpu.make_async_copy(
            stage.at[:, pl.ds(last, 1)], out_ref.at[:, pl.ds(last, 1)], sems.at[ARR + 1]
        )
        notes.start()

        def write_of(m):
            at = pl.ds(m * 2 * tiles, 2 * tiles)
            return pltpu.make_async_copy(stage.at[:, at], out_ref.at[:, at], sems.at[ARR])

        def clear(m, carry):
            def one(j, inner):
                stage[j, pl.ds(m * 2 * tiles, 2 * tiles)] = jnp.zeros((2 * tiles, TILE, HD), jnp.bfloat16)
                return inner

            return lax.fori_loop(used(m), pages, one, carry)

        lax.fori_loop(0, count, clear, 0)
        row = lax.broadcasted_iota(jnp.int32, (tiles, TILE, HD), 0) * TILE + lax.broadcasted_iota(
            jnp.int32, (tiles, TILE, HD), 1
        )

        def finish(m, carry):
            full = used(m)

            def one(j, inner):
                for copy in reads_of(m, j):
                    copy.wait()
                return inner

            lax.fori_loop(0, full, one, 0)
            rest = ctx[list_ref[m]] - (full - 1) * page
            for kind in range(2):
                at = pl.ds((m * 2 + kind) * tiles, tiles)
                edge = stage[full - 1, at]
                stage[full - 1, at] = jnp.where(row < rest, edge, jnp.zeros_like(edge))
            write_of(m).start()
            return carry

        def settle_writes(m, carry):
            write_of(m).wait()
            return carry

        lax.fori_loop(0, count, finish, 0)
        lax.fori_loop(0, count, settle_writes, 0)
        notes.wait()

    hbm = pl.BlockSpec(memory_space=pltpu.HBM)
    return pl.pallas_call(
        kernel,
        in_specs=[hbm] * 5,
        out_specs=hbm,
        scratch_shapes=[
            pltpu.SMEM((slots, pages), jnp.int32),
            pltpu.SMEM((slots,), jnp.int32),
            pltpu.SMEM((slots,), jnp.int32),
            pltpu.SMEM((slots,), jnp.int32),
            pltpu.SMEM((ARR + 1,), jnp.int32),
            pltpu.VMEM((ranks, last + 1, TILE, HD), jnp.bfloat16),
            pltpu.SemaphoreType.DMA((ARR + 2,)),
            pltpu.SemaphoreType.DMA((4,)),
        ],
        out_shape=jax.ShapeDtypeStruct((ranks, last + 1, TILE, HD), jnp.bfloat16),
        compiler_params=pltpu.CompilerParams(vmem_limit_bytes=56 * 1024 * 1024),
        name="pack_pages",
    )(page_table, context, remaining, move_to, pltpu.with_memory_space_constraint(pool, pltpu.HBM))


def relay_pages(source, received, going):
    ranks, rows = received.shape[:2]
    span = (rows - 1) // ARR
    more = going.shape[0]

    def kernel(src, got_ref, going_ref, out_ref):
        for d in range(ranks):
            for a in range(ARR):
                k = src[d * ARR + a]
                place = jnp.maximum(k, 0)
                block = got_ref[place // ARR, pl.ds((place & (ARR - 1)) * span, span)]
                out_ref[d, a * span : (a + 1) * span] = jnp.where(k >= 0, block, jnp.zeros_like(block))
            for c in range(more):
                out_ref[d, ARR * span + c] = going_ref[c, d * TILE : (d + 1) * TILE]

    vmem = pl.BlockSpec(memory_space=pltpu.VMEM)
    return pl.pallas_call(
        kernel,
        in_specs=[pl.BlockSpec(memory_space=pltpu.SMEM), vmem, vmem],
        out_specs=vmem,
        out_shape=jax.ShapeDtypeStruct((ranks, ARR * span + more, TILE, HD), jnp.bfloat16),
        compiler_params=pltpu.CompilerParams(vmem_limit_bytes=16 * 1024 * 1024),
        name="relay_pages",
    )(source, received, going)


def plan_relay(goals, slots, ranks):
    count = goals.shape[0]
    home = goals // slots
    before = (home[None, :] == home[:, None]) & (goals[None, :] < goals[:, None])
    order = jnp.sum(before.astype(jnp.int32), axis=1)
    target = home * ARR + order
    ids = jnp.arange(count, dtype=jnp.int32)
    hit = target[None, :] == jnp.arange(ranks * ARR, dtype=jnp.int32)[:, None]
    return jnp.max(jnp.where(hit, ids[None, :], -1), axis=1)


def old_pages(page_table, context, remaining, w_keyval, cache):
    slots, pages = page_table.shape
    page = cache.shape[2]

    def kernel(table, ctx, left, w_ref, cache_ref, old, w_out, sems, sem):
        weights = pltpu.make_async_copy(w_ref, w_out, sem)
        weights.start()

        def used(b):
            return jnp.where(left[b] > 0, lax.div(ctx[b] + page - 1, page), 0)

        def copy_page(b, j):
            return pltpu.make_async_copy(
                cache_ref.at[:, table[b, j]], old.at[b, :, pl.ds(j * page, page)], sems.at[b]
            )

        def fetch(b, carry):
            def one(j, inner):
                copy_page(b, j).start()
                return inner

            def clear(j, inner):
                old[b, 1, pl.ds(j * page, page)] = jnp.zeros((page, HD), jnp.bfloat16)
                return inner

            lax.fori_loop(0, used(b), one, 0)
            return lax.fori_loop(used(b), pages, clear, carry)

        def finish(b, carry):
            def one(j, inner):
                copy_page(b, j).wait()
                return inner

            return lax.fori_loop(0, used(b), one, carry)

        lax.fori_loop(0, slots, fetch, 0)
        lax.fori_loop(0, slots, finish, 0)
        weights.wait()

    smem = pl.BlockSpec(memory_space=pltpu.SMEM)
    hbm = pl.BlockSpec(memory_space=pltpu.HBM)
    vmem = pl.BlockSpec(memory_space=pltpu.VMEM)
    return pl.pallas_call(
        kernel,
        in_specs=[smem] * 3 + [hbm] * 2,
        out_specs=[vmem, vmem],
        scratch_shapes=[pltpu.SemaphoreType.DMA((slots,)), pltpu.SemaphoreType.DMA(())],
        out_shape=[
            pltpu.VMEM((slots, 2, pages * page, HD), cache.dtype),
            pltpu.VMEM(w_keyval.shape, w_keyval.dtype),
        ],
        compiler_params=pltpu.CompilerParams(vmem_limit_bytes=16 * 1024 * 1024),
        cost_estimate=pl.CostEstimate(flops=0, bytes_accessed=24 * 1024 * 1024, transcendentals=0),
        name="old_pages",
    )(page_table, context, remaining, *(pltpu.with_memory_space_constraint(x, pltpu.HBM) for x in (w_keyval, cache)))


def project_attend(
    context, remaining, shifts, parts, gain, w_query, w_keyval, b_query, b_keyval, cos, sin, pick, old
):
    slots, span = old.shape[0], old.shape[2]
    count = len(parts)
    rows, depth = parts[0].shape
    steps = rows // slots
    width = w_query.shape[1]
    wide = width + 2 * HD
    heads = width // HD
    sends = pick.shape[1]
    chunks = wide // HD
    pair = 8 // steps
    scale = 1.0 / math.sqrt(HD)
    model_width = count * depth

    def kernel(*refs):
        ctx, left = refs[:2]
        hid = refs[2 : 2 + count]
        (
            gain_ref, bq_ref, bkv_ref, cos_ref, sin_ref, pick_ref, wkv, old, wq_hbm,
            rows_ref, send_ref, acc, query, fresh, mixed, wq, sems,
        ) = refs[2 + count :]

        here = lax.axis_index("tensor").astype(jnp.int32)
        near = [lax.rem(here + count - 2 * k, count) for k in shifts]
        source = near + [place ^ 1 for place in near]
        half = depth // 2

        def weights_of(i, n):
            begin = pl.multiple_of(source[i] * depth + n * half, half)
            return pltpu.make_async_copy(
                wq_hbm.at[pl.ds(begin, half)], wq.at[pl.ds(i * depth + n * half, half)], sems.at[2 * i + n]
            )

        for i in range(count):
            for n in range(2):
                weights_of(i, n).start()

        squares = jnp.zeros((rows, 1), jnp.float32)
        for i in range(count):
            part = hid[i][...].astype(jnp.float32)
            normed = (part * gain_ref[source[i]].astype(jnp.float32)).astype(jnp.bfloat16)
            squares += jnp.sum(part * part, axis=1, keepdims=True)
            at = pl.ds(pl.multiple_of(source[i] * depth, depth), depth)
            sums = [jnp.dot(normed, wkv[kind, at], preferred_element_type=jnp.float32) for kind in range(2)]
            for n in range(2):
                weights_of(i, n).wait()
                sums.append(
                    jnp.dot(
                        normed[:, n * half : (n + 1) * half],
                        wq[i * depth + n * half : i * depth + (n + 1) * half],
                        preferred_element_type=jnp.float32,
                    )
                )
            key_sum, value_sum, first_half, second_half = sums
            for lanes, part_sum in (
                (slice(0, width), first_half + second_half),
                (slice(width, width + HD), key_sum),
                (slice(width + HD, wide), value_sum),
            ):
                if i:
                    acc[:, lanes] += part_sum
                else:
                    acc[:, lanes] = part_sum

        row_scale = lax.rsqrt(squares / model_width + norm_eps)
        cosine, sine = cos_ref[...], sin_ref[...]

        def rotate(x):
            return x * cosine + pltpu.roll(x, HD // 2, 1) * sine

        many = heads * 8
        for h in range(heads):
            at = slice(h * HD, (h + 1) * HD)
            q = rotate(acc[:, at] * row_scale + bq_ref[:, at].astype(jnp.float32))
            for p in range(rows // 8):
                query[p * many + h * 8 : p * many + (h + 1) * 8, :] = q[p * 8 : (p + 1) * 8, :]
        key = rotate(acc[:, width : width + HD] * row_scale + bkv_ref[0:1].astype(jnp.float32))
        value = acc[:, width + HD :] * row_scale + bkv_ref[1:2].astype(jnp.float32)
        fresh[0, :rows] = key.astype(jnp.bfloat16)
        fresh[1, :rows] = value.astype(jnp.bfloat16)
        fresh[:, rows:] = jnp.zeros((2, HD - rows, HD), jnp.bfloat16)
        row_of = lax.broadcasted_iota(jnp.int32, (rows, HD), 0)
        live_of = jnp.zeros((rows, HD), jnp.int32)
        for b in range(slots):
            live_of = jnp.where(row_of // steps == b, left[b], live_of)
        alive = row_of % steps < live_of
        mixed[:, width : width + HD] = jnp.where(alive, key, 0.0)
        mixed[:, width + HD :] = jnp.where(alive, value, 0.0)

        col = lax.broadcasted_iota(jnp.int32, (many, span), 1)
        new_col = lax.broadcasted_iota(jnp.int32, (many, HD), 1)
        line = lax.broadcasted_iota(jnp.int32, (many, HD), 0) % 8
        line_one = lax.broadcasted_iota(jnp.int32, (many, 1), 0) % 8
        for p in range(slots // pair):
            members = range(p * pair, (p + 1) * pair)
            q = query[p * many : (p + 1) * many, :].astype(jnp.bfloat16)

            def mine(values, at):
                out = values[0]
                for n in range(1, pair):
                    out = jnp.where(at >= n * steps, values[n], out)
                return out

            wide_line = jnp.broadcast_to(line_one, (many, span))
            scores = mine(
                [
                    lax.dot_general(q, old[b, 0], (((1,), (1,)), ((), ())), preferred_element_type=jnp.float32)
                    for b in members
                ],
                wide_line,
            )
            limit = mine([jnp.full((many, 1), ctx[b], jnp.int32) for b in members], line_one)
            scores = jnp.where(col < limit, scores * scale, masked_score)
            late = lax.dot_general(q, fresh[0], (((1,), (1,)), ((), ())), preferred_element_type=jnp.float32)
            since = new_col - p * 8
            seen = (since >= (line // steps) * steps) & (since <= line)
            late = jnp.where(seen, late * scale, masked_score)
            top = jnp.maximum(jnp.max(scores, axis=1, keepdims=True), jnp.max(late, axis=1, keepdims=True))
            scores = jnp.exp(scores - top)
            late = jnp.exp(late - top)
            rate = 1.0 / (jnp.sum(scores, axis=1, keepdims=True) + jnp.sum(late, axis=1, keepdims=True))
            scores = (scores * rate).astype(jnp.bfloat16)
            late = (late * rate).astype(jnp.bfloat16)
            out = mine(
                [jnp.dot(scores, old[b, 1], preferred_element_type=jnp.float32) for b in members], line
            )
            out = out + jnp.dot(late, fresh[1], preferred_element_type=jnp.float32)
            rest = mine([jnp.full((many, HD), left[b], jnp.int32) for b in members], line)
            out = jnp.where(line % steps < rest, out, 0.0)
            for h in range(heads):
                mixed[p * 8 : (p + 1) * 8, h * HD : (h + 1) * HD] = out[h * 8 : (h + 1) * 8]

        done_rows = mixed[...].astype(jnp.bfloat16)
        rows_ref[...] = done_rows
        column = lax.broadcasted_iota(jnp.int32, (rows, sends), 0)
        upper = lax.broadcasted_iota(jnp.int32, (rows, sends), 1) % TILE < TILE // 2
        chosen = pick_ref[...] == column
        first = jnp.where(chosen & upper, 1.0, 0.0).T.astype(jnp.bfloat16)
        second = jnp.where(chosen & jnp.logical_not(upper), 1.0, 0.0).T.astype(jnp.bfloat16)
        for c in range(chunks // 2):
            lanes = slice(2 * c * HD, (2 * c + 1) * HD)
            after = slice((2 * c + 1) * HD, (2 * c + 2) * HD)
            tile = jnp.dot(first, done_rows[:, lanes], preferred_element_type=jnp.float32) + jnp.dot(
                second, done_rows[:, after], preferred_element_type=jnp.float32
            )
            send_ref[c] = tile.astype(jnp.bfloat16)

    vmem = pl.BlockSpec(memory_space=pltpu.VMEM)
    smem = pl.BlockSpec(memory_space=pltpu.SMEM)
    hbm = pl.BlockSpec(memory_space=pltpu.HBM)
    return pl.pallas_call(
        kernel,
        in_specs=[smem] * 2 + [vmem] * (count + 8) + [hbm],
        out_specs=[vmem, vmem],
        scratch_shapes=[
            pltpu.VMEM((rows, wide), jnp.float32),
            pltpu.VMEM((rows * heads, HD), jnp.float32),
            pltpu.VMEM((2, HD, HD), jnp.bfloat16),
            pltpu.VMEM((rows, wide), jnp.float32),
            pltpu.VMEM((model_width, width), jnp.bfloat16),
            pltpu.SemaphoreType.DMA((2 * count,)),
        ],
        out_shape=[
            jax.ShapeDtypeStruct((rows, wide), jnp.bfloat16),
            jax.ShapeDtypeStruct((chunks // 2, sends, HD), jnp.bfloat16),
        ],
        compiler_params=pltpu.CompilerParams(vmem_limit_bytes=22 * 1024 * 1024),
        cost_estimate=pl.CostEstimate(
            flops=2 * rows * model_width * wide, bytes_accessed=32 * 1024 * 1024, transcendentals=rows * heads * span
        ),
        name="project_attend",
    )(
        context, remaining, *parts, gain, b_query, b_keyval, cos, sin, pick,
        *(pltpu.with_memory_space_constraint(x, pltpu.VMEM) for x in (w_keyval, old)),
        pltpu.with_memory_space_constraint(w_query, pltpu.HBM),
    )


def from_chips(rows):
    count = lax.axis_size("tensor")
    chips = count // 2
    shifts = [0] + list(dict.fromkeys(k for k in (1, chips - 1, *range(2, chips)) if 0 < k < chips))
    parts = [lax.ppermute(rows, "tensor", [(r, (r + 2 * k) % count) for r in range(count)]) if k else rows for k in shifts]
    return parts, shifts


def from_sibling(parts):
    count = lax.axis_size("tensor")
    return [lax.ppermute(part, "tensor", [(r, r ^ 1) for r in range(count)]) for part in parts]


def settle(landed, mine, take, pages, width):
    ranks, tiles = landed.shape[:2]
    rows, wide = mine.shape
    chunks = wide // HD
    span = (tiles - chunks // 2) // ARR
    part = span // 2
    slots = rows // STEPS

    def kernel(landed_ref, mine_ref, take_ref, out_ref, kv_ref, arrived_ref, sems):
        copies = [
            pltpu.make_async_copy(
                landed_ref.at[:, pl.ds(a * span + kind * part, part)], arrived_ref.at[kind, a], sems.at[2 * a + kind]
            )
            for a in range(ARR)
            for kind in range(2)
        ]
        for copy in copies:
            copy.start()
        index = take_ref[...]
        own = jnp.where(index == lax.broadcasted_iota(jnp.int32, (rows, rows), 0), 1.0, 0.0).T.astype(jnp.bfloat16)
        place = lax.broadcasted_iota(jnp.int32, (ranks * TILE, rows), 0)
        half = TILE // 2
        flat = rows + place // TILE * half + place % half
        upper = place % TILE < half
        hit = index == flat
        came = [
            jnp.where(hit & upper, 1.0, 0.0).T.astype(jnp.bfloat16),
            jnp.where(hit & jnp.logical_not(upper), 1.0, 0.0).T.astype(jnp.bfloat16),
        ]
        for c in range(chunks):
            lanes = slice(c * HD, (c + 1) * HD)
            got = landed_ref[:, ARR * span + c // 2].reshape(ranks * TILE, HD)
            final = jnp.dot(own, mine_ref[:, lanes], preferred_element_type=jnp.float32) + jnp.dot(
                came[c % 2], got, preferred_element_type=jnp.float32
            )
            final = final.reshape(slots, STEPS, HD).astype(jnp.bfloat16)
            if c < chunks - 2:
                out_ref[:, :, lanes] = final
            else:
                kv_ref[c - (chunks - 2)] = final
        for copy in copies:
            copy.wait()

    vmem = pl.BlockSpec(memory_space=pltpu.VMEM)
    return pl.pallas_call(
        kernel,
        in_specs=[vmem] * 3,
        out_specs=[vmem, vmem, pl.BlockSpec(memory_space=pltpu.HBM)],
        scratch_shapes=[pltpu.SemaphoreType.DMA((2 * ARR,))],
        out_shape=[
            jax.ShapeDtypeStruct((slots, STEPS, width), jnp.bfloat16),
            jax.ShapeDtypeStruct((2, slots, STEPS, HD), jnp.bfloat16),
            jax.ShapeDtypeStruct((2, ARR, ranks, part, TILE, HD), jnp.bfloat16),
        ],
        compiler_params=pltpu.CompilerParams(vmem_limit_bytes=16 * 1024 * 1024),
        name="settle",
    )(landed, mine, take)


def local(
    hidden, norm_gain, w_query, w_keyval, b_query, b_keyval, cache, page_table, context, remaining, move_to
):
    slots, steps, depth = hidden.shape
    ranks = lax.axis_size("dp")
    rank = lax.axis_index("dp").astype(jnp.int32)
    page = cache.shape[2]
    pages = page_table.shape[1]
    width = w_query.shape[1]
    rows = slots * steps
    ids = jnp.arange(slots, dtype=jnp.int32)

    sent = pack_pages(page_table, context, remaining, move_to, cache, ranks)
    sent, hidden = lax.optimization_barrier((sent, hidden))
    received = lax.all_to_all(sent, "dp", 0, 0, tiled=True)

    staying = move_to == ids + rank * slots
    leaving = jnp.logical_not(staying) & (remaining > 0)
    coming = jnp.logical_not(staying) & (remaining == 0)
    there = move_to // slots
    same = there[None, :] == there[:, None]
    leave_order = jnp.sum((same & leaving[None, :] & (ids[None, :] < ids[:, None])).astype(jnp.int32), axis=1)
    come_order = jnp.sum(
        (same & coming[None, :] & (move_to[None, :] < move_to[:, None])).astype(jnp.int32), axis=1
    )
    place = jnp.where(leaving, there * CAP + leave_order, -1)
    hit = place[None, :] == jnp.arange(ranks * CAP, dtype=jnp.int32)[:, None]
    slot_of = jnp.max(jnp.where(hit, ids[None, :], -1), axis=1)
    step_ids = jnp.arange(steps, dtype=jnp.int32)
    pick = jnp.where(slot_of[:, None] >= 0, slot_of[:, None] * steps + step_ids[None, :], -1)
    pick = jnp.broadcast_to(pick.reshape(ranks, 1, CAP * steps), (ranks, 2, CAP * steps)).reshape(1, -1)

    half = HD // 2
    inverse = rope_base ** (-(jnp.arange(half, dtype=jnp.float32) * (2.0 / HD)))
    positions = (context[:, None] + step_ids[None, :]).reshape(-1).astype(jnp.float32)
    angles = positions[:, None] * inverse[None, :]
    cos, sin = jnp.cos(angles), jnp.sin(angles)
    cos = jnp.concatenate([cos, cos], axis=1)
    sin = jnp.concatenate([-sin, sin], axis=1)

    def attend(hidden):
        near, shifts = from_chips(hidden.reshape(rows, depth))
        old, weights_keyval = old_pages(page_table, context, remaining, w_keyval, cache)
        small = (
            norm_gain.reshape(-1, 1, depth), b_query.reshape(1, width), b_keyval, cos, sin, pick, context, remaining,
        )
        near, old, weights_keyval, small = lax.optimization_barrier((near, old, weights_keyval, small))
        gain, bias, bias_keyval, cosine, sine, picked, tokens, left = small
        far = from_sibling(near)
        return tuple(
            project_attend(
                tokens, left, shifts, near + far, gain, w_query, weights_keyval, bias, bias_keyval, cosine, sine,
                picked, old,
            )
        )

    def nothing(hidden):
        wide = width + 2 * HD
        return jnp.zeros((rows, wide), jnp.bfloat16), jnp.zeros((wide // HD // 2, pick.shape[1], HD), jnp.bfloat16)

    mine, going = lax.cond(context[0] > 0, attend, nothing, hidden)
    base = jnp.where(staying, ids * steps, jnp.where(coming, rows + (there * CAP + come_order) * steps, -steps))
    take = (base[:, None] + step_ids[None, :]).reshape(1, -1)
    received, mine, going, take = lax.optimization_barrier((received, mine, going, take))
    goals = received[:, -1, 0, :ARR].astype(jnp.int32).reshape(-1)
    relayed = relay_pages(plan_relay(goals, slots, ranks), received, going)
    landed = lax.all_to_all(relayed, "dp", 0, 0, tiled=True)
    attended, new_keyval, arrived = settle(landed, mine, take, pages, width)
    return attended, new_keyval, arrived.reshape(2, ARR, pages * page, HD)


def solution(mesh):
    in_specs = (
        P("dp", None, "tensor"),
        P(),
        P(None, "tensor"),
        P(None, None, "tensor"),
        P("tensor"),
        P(None, "tensor"),
        P(None, "dp", None, "tensor"),
        P("dp", None),
        P("dp"),
        P("dp"),
        P("dp"),
    )
    out_specs = (
        P("dp", None, "tensor"),
        P(None, "dp", None, "tensor"),
        P(None, "dp", None, "tensor"),
    )
    return jax.shard_map(local, mesh=mesh, in_specs=in_specs, out_specs=out_specs, check_vma=False)
```

```python
import math

import jax
import jax.numpy as jnp
from jax import lax
from jax.experimental import pallas as pl
from jax.experimental.pallas import tpu as pltpu
from jax.sharding import PartitionSpec as P

HD = 128
ARR = 4
CAP = 2
TILE = 16
STEPS = 4

rope_base = 1000000.0
norm_eps = 1e-06
masked_score = -1e30


def pack_pages(page_table, context, remaining, move_to, cache, ranks):
    slots, pages = page_table.shape
    page = cache.shape[2]
    tiles = page // TILE
    pool = cache.reshape(2, cache.shape[1], tiles, TILE, HD)
    last = ARR * 2 * tiles

    def kernel(
        table_hbm, ctx_hbm, left_hbm, goal_hbm, pool_ref, out_ref, table, ctx, left, goal, list_ref, stage, sems, small,
    ):
        reads = [
            pltpu.make_async_copy(src, dst, small.at[n])
            for n, (src, dst) in enumerate(
                ((table_hbm, table), (ctx_hbm, ctx), (left_hbm, left), (goal_hbm, goal))
            )
        ]
        for read in reads:
            read.start()
        for read in reads:
            read.wait()
        first = lax.axis_index("dp").astype(jnp.int32) * slots

        for m in range(ARR):
            list_ref[m] = 0
        count = jnp.int32(0)
        for b in range(slots):
            leaves = jnp.logical_and(left[b] > 0, goal[b] != first + b)
            list_ref[jnp.where(leaves, jnp.minimum(count, ARR - 1), ARR)] = b
            count = count + leaves.astype(jnp.int32)
        count = jnp.minimum(count, ARR)

        def used(m):
            return lax.div(ctx[list_ref[m]] + page - 1, page)

        def reads_of(m, j):
            b = list_ref[m]
            return [
                pltpu.make_async_copy(
                    pool_ref.at[kind, table[b, j]], stage.at[j, pl.ds((m * 2 + kind) * tiles, tiles)], sems.at[m]
                )
                for kind in range(2)
            ]

        def start(m, carry):
            def one(j, inner):
                for copy in reads_of(m, j):
                    copy.start()
                return inner

            return lax.fori_loop(0, used(m), one, carry)

        lax.fori_loop(0, count, start, 0)
        lane = lax.broadcasted_iota(jnp.int32, (TILE, HD), 1)
        note_tile = jnp.full((TILE, HD), 512, jnp.int32)
        for m in range(ARR):
            note_tile = jnp.where(lane == m, jnp.where(m < count, goal[list_ref[m]], 512), note_tile)
        note_tile = note_tile.astype(jnp.float32).astype(jnp.bfloat16)
        for j in range(ranks):
            stage[j, last] = note_tile
        notes = pltpu.make_async_copy(
            stage.at[:, pl.ds(last, 1)], out_ref.at[:, pl.ds(last, 1)], sems.at[ARR + 1]
        )
        notes.start()

        def write_of(m):
            at = pl.ds(m * 2 * tiles, 2 * tiles)
            return pltpu.make_async_copy(stage.at[:, at], out_ref.at[:, at], sems.at[ARR])

        def clear(m, carry):
            def one(j, inner):
                stage[j, pl.ds(m * 2 * tiles, 2 * tiles)] = jnp.zeros((2 * tiles, TILE, HD), jnp.bfloat16)
                return inner

            return lax.fori_loop(used(m), pages, one, carry)

        lax.fori_loop(0, count, clear, 0)
        row = lax.broadcasted_iota(jnp.int32, (tiles, TILE, HD), 0) * TILE + lax.broadcasted_iota(
            jnp.int32, (tiles, TILE, HD), 1
        )

        def finish(m, carry):
            full = used(m)

            def one(j, inner):
                for copy in reads_of(m, j):
                    copy.wait()
                return inner

            lax.fori_loop(0, full, one, 0)
            rest = ctx[list_ref[m]] - (full - 1) * page
            for kind in range(2):
                at = pl.ds((m * 2 + kind) * tiles, tiles)
                edge = stage[full - 1, at]
                stage[full - 1, at] = jnp.where(row < rest, edge, jnp.zeros_like(edge))
            write_of(m).start()
            return carry

        def settle_writes(m, carry):
            write_of(m).wait()
            return carry

        lax.fori_loop(0, count, finish, 0)
        lax.fori_loop(0, count, settle_writes, 0)
        notes.wait()

    hbm = pl.BlockSpec(memory_space=pltpu.HBM)
    return pl.pallas_call(
        kernel,
        in_specs=[hbm] * 5,
        out_specs=hbm,
        scratch_shapes=[
            pltpu.SMEM((slots, pages), jnp.int32),
            pltpu.SMEM((slots,), jnp.int32),
            pltpu.SMEM((slots,), jnp.int32),
            pltpu.SMEM((slots,), jnp.int32),
            pltpu.SMEM((ARR + 1,), jnp.int32),
            pltpu.VMEM((ranks, last + 1, TILE, HD), jnp.bfloat16),
            pltpu.SemaphoreType.DMA((ARR + 2,)),
            pltpu.SemaphoreType.DMA((4,)),
        ],
        out_shape=jax.ShapeDtypeStruct((ranks, last + 1, TILE, HD), jnp.bfloat16),
        compiler_params=pltpu.CompilerParams(vmem_limit_bytes=56 * 1024 * 1024),
        name="pack_pages",
    )(page_table, context, remaining, move_to, pltpu.with_memory_space_constraint(pool, pltpu.HBM))


def relay_pages(source, received, going):
    ranks, rows = received.shape[:2]
    span = (rows - 1) // ARR
    more = going.shape[0]

    def kernel(src, got_ref, going_ref, out_ref):
        for d in range(ranks):
            for a in range(ARR):
                k = src[d * ARR + a]
                place = jnp.maximum(k, 0)
                block = got_ref[place // ARR, pl.ds((place & (ARR - 1)) * span, span)]
                out_ref[d, a * span : (a + 1) * span] = jnp.where(k >= 0, block, jnp.zeros_like(block))
            for c in range(more):
                out_ref[d, ARR * span + c] = going_ref[c, d * TILE : (d + 1) * TILE]

    vmem = pl.BlockSpec(memory_space=pltpu.VMEM)
    return pl.pallas_call(
        kernel,
        in_specs=[pl.BlockSpec(memory_space=pltpu.SMEM), vmem, vmem],
        out_specs=vmem,
        out_shape=jax.ShapeDtypeStruct((ranks, ARR * span + more, TILE, HD), jnp.bfloat16),
        compiler_params=pltpu.CompilerParams(vmem_limit_bytes=16 * 1024 * 1024),
        name="relay_pages",
    )(source, received, going)


def plan_relay(goals, slots, ranks):
    count = goals.shape[0]
    home = goals // slots
    before = (home[None, :] == home[:, None]) & (goals[None, :] < goals[:, None])
    order = jnp.sum(before.astype(jnp.int32), axis=1)
    target = home * ARR + order
    ids = jnp.arange(count, dtype=jnp.int32)
    hit = target[None, :] == jnp.arange(ranks * ARR, dtype=jnp.int32)[:, None]
    return jnp.max(jnp.where(hit, ids[None, :], -1), axis=1)


def old_pages(page_table, context, remaining, w_keyval, cache):
    slots, pages = page_table.shape
    page = cache.shape[2]

    def kernel(table, ctx, left, w_ref, cache_ref, old, w_out, sems, sem):
        weights = pltpu.make_async_copy(w_ref, w_out, sem)
        weights.start()

        def used(b):
            return jnp.where(left[b] > 0, lax.div(ctx[b] + page - 1, page), 0)

        def copy_page(b, j):
            return pltpu.make_async_copy(
                cache_ref.at[:, table[b, j]], old.at[b, :, pl.ds(j * page, page)], sems.at[b]
            )

        def fetch(b, carry):
            def one(j, inner):
                copy_page(b, j).start()
                return inner

            def clear(j, inner):
                old[b, 1, pl.ds(j * page, page)] = jnp.zeros((page, HD), jnp.bfloat16)
                return inner

            lax.fori_loop(0, used(b), one, 0)
            return lax.fori_loop(used(b), pages, clear, carry)

        def finish(b, carry):
            def one(j, inner):
                copy_page(b, j).wait()
                return inner

            return lax.fori_loop(0, used(b), one, carry)

        lax.fori_loop(0, slots, fetch, 0)
        lax.fori_loop(0, slots, finish, 0)
        weights.wait()

    smem = pl.BlockSpec(memory_space=pltpu.SMEM)
    hbm = pl.BlockSpec(memory_space=pltpu.HBM)
    vmem = pl.BlockSpec(memory_space=pltpu.VMEM)
    return pl.pallas_call(
        kernel,
        in_specs=[smem] * 3 + [hbm] * 2,
        out_specs=[vmem, vmem],
        scratch_shapes=[pltpu.SemaphoreType.DMA((slots,)), pltpu.SemaphoreType.DMA(())],
        out_shape=[
            pltpu.VMEM((slots, 2, pages * page, HD), cache.dtype),
            pltpu.VMEM(w_keyval.shape, w_keyval.dtype),
        ],
        compiler_params=pltpu.CompilerParams(vmem_limit_bytes=16 * 1024 * 1024),
        cost_estimate=pl.CostEstimate(flops=0, bytes_accessed=24 * 1024 * 1024, transcendentals=0),
        name="old_pages",
    )(page_table, context, remaining, *(pltpu.with_memory_space_constraint(x, pltpu.HBM) for x in (w_keyval, cache)))


def project_attend(
    context, remaining, shifts, parts, gain, w_query, w_keyval, b_query, b_keyval, cos, sin, pick, old
):
    slots, span = old.shape[0], old.shape[2]
    count = len(parts)
    rows, depth = parts[0].shape
    steps = rows // slots
    width = w_query.shape[1]
    wide = width + 2 * HD
    heads = width // HD
    sends = pick.shape[1]
    chunks = wide // HD
    pair = 8 // steps
    scale = 1.0 / math.sqrt(HD)
    model_width = count * depth

    def kernel(*refs):
        ctx, left = refs[:2]
        hid = refs[2 : 2 + count]
        (
            gain_ref, bq_ref, bkv_ref, cos_ref, sin_ref, pick_ref, wkv, old, wq_hbm,
            rows_ref, send_ref, acc, query, fresh, mixed, wq, sems,
        ) = refs[2 + count :]

        here = lax.axis_index("tensor").astype(jnp.int32)
        near = [lax.rem(here + count - 2 * k, count) for k in shifts]
        source = near + [place ^ 1 for place in near]
        half = depth // 2

        def weights_of(i, n):
            begin = pl.multiple_of(source[i] * depth + n * half, half)
            return pltpu.make_async_copy(
                wq_hbm.at[pl.ds(begin, half)], wq.at[pl.ds(i * depth + n * half, half)], sems.at[2 * i + n]
            )

        for i in range(count):
            for n in range(2):
                weights_of(i, n).start()

        squares = jnp.zeros((rows, 1), jnp.float32)
        for i in range(count):
            part = hid[i][...].astype(jnp.float32)
            normed = (part * gain_ref[source[i]].astype(jnp.float32)).astype(jnp.bfloat16)
            squares += jnp.sum(part * part, axis=1, keepdims=True)
            at = pl.ds(pl.multiple_of(source[i] * depth, depth), depth)
            sums = [jnp.dot(normed, wkv[kind, at], preferred_element_type=jnp.float32) for kind in range(2)]
            for n in range(2):
                weights_of(i, n).wait()
                sums.append(
                    jnp.dot(
                        normed[:, n * half : (n + 1) * half],
                        wq[i * depth + n * half : i * depth + (n + 1) * half],
                        preferred_element_type=jnp.float32,
                    )
                )
            key_sum, value_sum, first_half, second_half = sums
            for lanes, part_sum in (
                (slice(0, width), first_half + second_half),
                (slice(width, width + HD), key_sum),
                (slice(width + HD, wide), value_sum),
            ):
                if i:
                    acc[:, lanes] += part_sum
                else:
                    acc[:, lanes] = part_sum

        row_scale = lax.rsqrt(squares / model_width + norm_eps)
        cosine, sine = cos_ref[...], sin_ref[...]

        def rotate(x):
            return x * cosine + pltpu.roll(x, HD // 2, 1) * sine

        many = heads * 8
        for h in range(heads):
            at = slice(h * HD, (h + 1) * HD)
            q = rotate(acc[:, at] * row_scale + bq_ref[:, at].astype(jnp.float32))
            for p in range(rows // 8):
                query[p * many + h * 8 : p * many + (h + 1) * 8, :] = q[p * 8 : (p + 1) * 8, :]
        key = rotate(acc[:, width : width + HD] * row_scale + bkv_ref[0:1].astype(jnp.float32))
        value = acc[:, width + HD :] * row_scale + bkv_ref[1:2].astype(jnp.float32)
        fresh[0, :rows] = key.astype(jnp.bfloat16)
        fresh[1, :rows] = value.astype(jnp.bfloat16)
        fresh[:, rows:] = jnp.zeros((2, HD - rows, HD), jnp.bfloat16)
        row_of = lax.broadcasted_iota(jnp.int32, (rows, HD), 0)
        live_of = jnp.zeros((rows, HD), jnp.int32)
        for b in range(slots):
            live_of = jnp.where(row_of // steps == b, left[b], live_of)
        alive = row_of % steps < live_of
        mixed[:, width : width + HD] = jnp.where(alive, key, 0.0)
        mixed[:, width + HD :] = jnp.where(alive, value, 0.0)

        col = lax.broadcasted_iota(jnp.int32, (many, span), 1)
        new_col = lax.broadcasted_iota(jnp.int32, (many, HD), 1)
        line = lax.broadcasted_iota(jnp.int32, (many, HD), 0) % 8
        line_one = lax.broadcasted_iota(jnp.int32, (many, 1), 0) % 8
        for p in range(slots // pair):
            members = range(p * pair, (p + 1) * pair)
            q = query[p * many : (p + 1) * many, :].astype(jnp.bfloat16)

            def mine(values, at):
                out = values[0]
                for n in range(1, pair):
                    out = jnp.where(at >= n * steps, values[n], out)
                return out

            wide_line = jnp.broadcast_to(line_one, (many, span))
            scores = mine(
                [
                    lax.dot_general(q, old[b, 0], (((1,), (1,)), ((), ())), preferred_element_type=jnp.float32)
                    for b in members
                ],
                wide_line,
            )
            limit = mine([jnp.full((many, 1), ctx[b], jnp.int32) for b in members], line_one)
            scores = jnp.where(col < limit, scores * scale, masked_score)
            late = lax.dot_general(q, fresh[0], (((1,), (1,)), ((), ())), preferred_element_type=jnp.float32)
            since = new_col - p * 8
            seen = (since >= (line // steps) * steps) & (since <= line)
            late = jnp.where(seen, late * scale, masked_score)
            top = jnp.maximum(jnp.max(scores, axis=1, keepdims=True), jnp.max(late, axis=1, keepdims=True))
            scores = jnp.exp(scores - top)
            late = jnp.exp(late - top)
            rate = 1.0 / (jnp.sum(scores, axis=1, keepdims=True) + jnp.sum(late, axis=1, keepdims=True))
            scores = (scores * rate).astype(jnp.bfloat16)
            late = (late * rate).astype(jnp.bfloat16)
            out = mine(
                [jnp.dot(scores, old[b, 1], preferred_element_type=jnp.float32) for b in members], line
            )
            out = out + jnp.dot(late, fresh[1], preferred_element_type=jnp.float32)
            rest = mine([jnp.full((many, HD), left[b], jnp.int32) for b in members], line)
            out = jnp.where(line % steps < rest, out, 0.0)
            for h in range(heads):
                mixed[p * 8 : (p + 1) * 8, h * HD : (h + 1) * HD] = out[h * 8 : (h + 1) * 8]

        done_rows = mixed[...].astype(jnp.bfloat16)
        rows_ref[...] = done_rows
        column = lax.broadcasted_iota(jnp.int32, (rows, sends), 0)
        upper = lax.broadcasted_iota(jnp.int32, (rows, sends), 1) % TILE < TILE // 2
        chosen = pick_ref[...] == column
        first = jnp.where(chosen & upper, 1.0, 0.0).T.astype(jnp.bfloat16)
        second = jnp.where(chosen & jnp.logical_not(upper), 1.0, 0.0).T.astype(jnp.bfloat16)
        for c in range(chunks // 2):
            lanes = slice(2 * c * HD, (2 * c + 1) * HD)
            after = slice((2 * c + 1) * HD, (2 * c + 2) * HD)
            tile = jnp.dot(first, done_rows[:, lanes], preferred_element_type=jnp.float32) + jnp.dot(
                second, done_rows[:, after], preferred_element_type=jnp.float32
            )
            send_ref[c] = tile.astype(jnp.bfloat16)

    vmem = pl.BlockSpec(memory_space=pltpu.VMEM)
    smem = pl.BlockSpec(memory_space=pltpu.SMEM)
    hbm = pl.BlockSpec(memory_space=pltpu.HBM)
    return pl.pallas_call(
        kernel,
        in_specs=[smem] * 2 + [vmem] * (count + 8) + [hbm],
        out_specs=[vmem, vmem],
        scratch_shapes=[
            pltpu.VMEM((rows, wide), jnp.float32),
            pltpu.VMEM((rows * heads, HD), jnp.float32),
            pltpu.VMEM((2, HD, HD), jnp.bfloat16),
            pltpu.VMEM((rows, wide), jnp.float32),
            pltpu.VMEM((model_width, width), jnp.bfloat16),
            pltpu.SemaphoreType.DMA((2 * count,)),
        ],
        out_shape=[
            jax.ShapeDtypeStruct((rows, wide), jnp.bfloat16),
            jax.ShapeDtypeStruct((chunks // 2, sends, HD), jnp.bfloat16),
        ],
        compiler_params=pltpu.CompilerParams(vmem_limit_bytes=22 * 1024 * 1024),
        cost_estimate=pl.CostEstimate(
            flops=2 * rows * model_width * wide, bytes_accessed=32 * 1024 * 1024, transcendentals=rows * heads * span
        ),
        name="project_attend",
    )(
        context, remaining, *parts, gain, b_query, b_keyval, cos, sin, pick,
        *(pltpu.with_memory_space_constraint(x, pltpu.VMEM) for x in (w_keyval, old)),
        pltpu.with_memory_space_constraint(w_query, pltpu.HBM),
    )


def from_chips(rows):
    count = lax.axis_size("tensor")
    chips = count // 2
    shifts = [0] + list(dict.fromkeys(k for k in (1, chips - 1, *range(2, chips)) if 0 < k < chips))
    parts = [lax.ppermute(rows, "tensor", [(r, (r + 2 * k) % count) for r in range(count)]) if k else rows for k in shifts]
    return parts, shifts


def from_sibling(parts):
    count = lax.axis_size("tensor")
    return [lax.ppermute(part, "tensor", [(r, r ^ 1) for r in range(count)]) for part in parts]


def settle(landed, mine, take, pages, width):
    ranks, tiles = landed.shape[:2]
    rows, wide = mine.shape
    chunks = wide // HD
    span = (tiles - chunks // 2) // ARR
    part = span // 2
    slots = rows // STEPS

    def kernel(landed_ref, mine_ref, take_ref, out_hbm, kv_hbm, arrived_ref, out_ref, kv_ref, sems):
        copies = [
            pltpu.make_async_copy(
                landed_ref.at[:, pl.ds(a * span + kind * part, part)], arrived_ref.at[kind, a], sems.at[2 * a + kind]
            )
            for a in range(ARR)
            for kind in range(2)
        ]
        for copy in copies:
            copy.start()
        index = take_ref[...]
        own = jnp.where(index == lax.broadcasted_iota(jnp.int32, (rows, rows), 0), 1.0, 0.0).T.astype(jnp.bfloat16)
        place = lax.broadcasted_iota(jnp.int32, (ranks * TILE, rows), 0)
        half = TILE // 2
        flat = rows + place // TILE * half + place % half
        upper = place % TILE < half
        hit = index == flat
        came = [
            jnp.where(hit & upper, 1.0, 0.0).T.astype(jnp.bfloat16),
            jnp.where(hit & jnp.logical_not(upper), 1.0, 0.0).T.astype(jnp.bfloat16),
        ]
        for c in range(chunks):
            lanes = slice(c * HD, (c + 1) * HD)
            got = landed_ref[:, ARR * span + c // 2].reshape(ranks * TILE, HD)
            final = jnp.dot(own, mine_ref[:, lanes], preferred_element_type=jnp.float32) + jnp.dot(
                came[c % 2], got, preferred_element_type=jnp.float32
            )
            final = final.reshape(slots, STEPS, HD).astype(jnp.bfloat16)
            if c < chunks - 2:
                out_ref[:, :, lanes] = final
            else:
                kv_ref[c - (chunks - 2)] = final
        rows_out = [
            pltpu.make_async_copy(out_ref, out_hbm, sems.at[2 * ARR]),
            pltpu.make_async_copy(kv_ref, kv_hbm, sems.at[2 * ARR + 1]),
        ]
        for copy in rows_out:
            copy.start()
        for copy in copies + rows_out:
            copy.wait()

    vmem = pl.BlockSpec(memory_space=pltpu.VMEM)
    return pl.pallas_call(
        kernel,
        in_specs=[vmem] * 3,
        out_specs=[pl.BlockSpec(memory_space=pltpu.HBM)] * 3,
        scratch_shapes=[
            pltpu.VMEM((slots, STEPS, width), jnp.bfloat16),
            pltpu.VMEM((2, slots, STEPS, HD), jnp.bfloat16),
            pltpu.SemaphoreType.DMA((2 * ARR + 2,)),
        ],
        out_shape=[
            jax.ShapeDtypeStruct((slots, STEPS, width), jnp.bfloat16),
            jax.ShapeDtypeStruct((2, slots, STEPS, HD), jnp.bfloat16),
            jax.ShapeDtypeStruct((2, ARR, ranks, part, TILE, HD), jnp.bfloat16),
        ],
        compiler_params=pltpu.CompilerParams(vmem_limit_bytes=16 * 1024 * 1024),
        name="settle",
    )(landed, mine, take)


def local(
    hidden, norm_gain, w_query, w_keyval, b_query, b_keyval, cache, page_table, context, remaining, move_to
):
    slots, steps, depth = hidden.shape
    ranks = lax.axis_size("dp")
    rank = lax.axis_index("dp").astype(jnp.int32)
    page = cache.shape[2]
    pages = page_table.shape[1]
    width = w_query.shape[1]
    rows = slots * steps
    ids = jnp.arange(slots, dtype=jnp.int32)

    sent = pack_pages(page_table, context, remaining, move_to, cache, ranks)
    sent, hidden = lax.optimization_barrier((sent, hidden))
    received = lax.all_to_all(sent, "dp", 0, 0, tiled=True)

    staying = move_to == ids + rank * slots
    leaving = jnp.logical_not(staying) & (remaining > 0)
    coming = jnp.logical_not(staying) & (remaining == 0)
    there = move_to // slots
    same = there[None, :] == there[:, None]
    leave_order = jnp.sum((same & leaving[None, :] & (ids[None, :] < ids[:, None])).astype(jnp.int32), axis=1)
    come_order = jnp.sum(
        (same & coming[None, :] & (move_to[None, :] < move_to[:, None])).astype(jnp.int32), axis=1
    )
    place = jnp.where(leaving, there * CAP + leave_order, -1)
    hit = place[None, :] == jnp.arange(ranks * CAP, dtype=jnp.int32)[:, None]
    slot_of = jnp.max(jnp.where(hit, ids[None, :], -1), axis=1)
    step_ids = jnp.arange(steps, dtype=jnp.int32)
    pick = jnp.where(slot_of[:, None] >= 0, slot_of[:, None] * steps + step_ids[None, :], -1)
    pick = jnp.broadcast_to(pick.reshape(ranks, 1, CAP * steps), (ranks, 2, CAP * steps)).reshape(1, -1)

    half = HD // 2
    inverse = rope_base ** (-(jnp.arange(half, dtype=jnp.float32) * (2.0 / HD)))
    positions = (context[:, None] + step_ids[None, :]).reshape(-1).astype(jnp.float32)
    angles = positions[:, None] * inverse[None, :]
    cos, sin = jnp.cos(angles), jnp.sin(angles)
    cos = jnp.concatenate([cos, cos], axis=1)
    sin = jnp.concatenate([-sin, sin], axis=1)

    def attend(hidden):
        near, shifts = from_chips(hidden.reshape(rows, depth))
        old, weights_keyval = old_pages(page_table, context, remaining, w_keyval, cache)
        small = (
            norm_gain.reshape(-1, 1, depth), b_query.reshape(1, width), b_keyval, cos, sin, pick, context, remaining,
        )
        near, old, weights_keyval, small = lax.optimization_barrier((near, old, weights_keyval, small))
        gain, bias, bias_keyval, cosine, sine, picked, tokens, left = small
        far = from_sibling(near)
        return tuple(
            project_attend(
                tokens, left, shifts, near + far, gain, w_query, weights_keyval, bias, bias_keyval, cosine, sine,
                picked, old,
            )
        )

    def nothing(hidden):
        wide = width + 2 * HD
        return jnp.zeros((rows, wide), jnp.bfloat16), jnp.zeros((wide // HD // 2, pick.shape[1], HD), jnp.bfloat16)

    mine, going = lax.cond(context[0] > 0, attend, nothing, hidden)
    base = jnp.where(staying, ids * steps, jnp.where(coming, rows + (there * CAP + come_order) * steps, -steps))
    take = (base[:, None] + step_ids[None, :]).reshape(1, -1)
    received, mine, going, take = lax.optimization_barrier((received, mine, going, take))
    goals = received[:, -1, 0, :ARR].astype(jnp.int32).reshape(-1)
    relayed = relay_pages(plan_relay(goals, slots, ranks), received, going)
    landed = lax.all_to_all(relayed, "dp", 0, 0, tiled=True)
    attended, new_keyval, arrived = settle(landed, mine, take, pages, width)
    return attended, new_keyval, arrived.reshape(2, ARR, pages * page, HD)


def solution(mesh):
    in_specs = (
        P("dp", None, "tensor"),
        P(),
        P(None, "tensor"),
        P(None, None, "tensor"),
        P("tensor"),
        P(None, "tensor"),
        P(None, "dp", None, "tensor"),
        P("dp", None),
        P("dp"),
        P("dp"),
        P("dp"),
    )
    out_specs = (
        P("dp", None, "tensor"),
        P(None, "dp", None, "tensor"),
        P(None, "dp", None, "tensor"),
    )
    return jax.shard_map(local, mesh=mesh, in_specs=in_specs, out_specs=out_specs, check_vma=False)
```
